512 devices in a mesh: blk: 32 (over z_hi, y), uly: 8 (over x, core), rep: 2 (over z_lo).
Axes of the slice: x: 4, y: 8, z: 8 (z_hi: 4, z_lo: 2; z = z_hi * 2 + z_lo), core: 2. Of those that a mesh axis runs over, the one named last changes fastest.
Arguments:
- query_mantissa: bfloat16 [65536, 4096], P(('rep', 'blk', 'uly')), parts along dimension 0, may hold values from -8 to 8
- key_mantissa: bfloat16 [65536, 4096], P(('rep', 'blk', 'uly')), parts along dimension 0, may hold values from -16 to 16
- value_mantissa: bfloat16 [65536, 4096], P(('rep', 'blk', 'uly')), parts along dimension 0, may hold values from -48 to 48
- query_exponent: int32 [65536, 32], P(('rep', 'blk', 'uly')), parts along dimension 0, may hold values from -1 to 1
- key_exponent: int32 [65536, 32], P(('rep', 'blk', 'uly')), parts along dimension 0, may hold values from -1 to 1
- value_exponent: int32 [65536, 32], P(('rep', 'blk', 'uly')), parts along dimension 0, may hold values from -1 to 1
- merge_map: int32 [65536], P(('rep', 'blk', 'uly')), parts along dimension 0, may hold values from 0 to 7, as said below
Outputs:
- attended: bfloat16 [65536, 4096], P(('rep', 'blk', 'uly')), parts along dimension 0
The draws below stay inside these ranges and needn't reach their ends.
There are 2 independent parts, one for each index of `rep`. The reference program is written for one: setup_inputs(seed, part) draws one part's arguments, and reference() takes and returns one part's arrays. A program takes and returns all parts, laid end to end along the dimension named above; each array names one. Nothing has to cross between parts.
Inputs may be any that keep to these rules, and one draw needn't show every extreme that they name: `merge_map`: within each aligned block of 128 tokens (one device's tokens) every value from 0 to 7 occurs at least once.
All inputs are finite; a program needn't handle non-finite values.
Results may differ from the reference program's by a relative error of at most 0.012.
The reference program's roundings to bfloat16 on the way count: a program that leaves them out, or rounds other values in their place, can miss the bound.
Values may be sent and summed in bfloat16 or wider, within the bound.
No kernel may reach another device: no remote copies, remote signals or barrier semaphores. Data moves between devices by JAX's collectives and lax.ppermute only.
A program may use at most 64 MiB of HBM per device.

```python
import math
import jax
import jax.numpy as jnp
from jax import lax

HD = 128
HEADS = 32
TOK_DEV = 128
HW = 4096
MERGED_DEV = 8
TOKENS = 32768
SLOTS = 2048


def draw_query_mantissa(key, part):
    key = jax.random.fold_in(key, 11)
    first_key = jax.random.fold_in(key, 0)
    result = jnp.clip(2.0 * jax.random.normal(first_key, (TOKENS, HW), jnp.float32), -8.0, 8.0)
    return result.astype(jnp.bfloat16)


def draw_key_mantissa(key, part):
    key = jax.random.fold_in(key, 23)
    first_key = jax.random.fold_in(key, 0)
    result = jnp.clip(4.0 * jax.random.normal(first_key, (TOKENS, HW), jnp.float32), -16.0, 16.0)
    return result.astype(jnp.bfloat16)


def draw_merge_map(key, part):
    key = jax.random.fold_in(key, 5)
    block_keys = jax.random.split(key, TOKENS // TOK_DEV)

    def one_block(block_key):
        fill_key, order_key = jax.random.split(block_key)
        every_slot = jnp.arange(MERGED_DEV, dtype=jnp.int32)
        further = jax.random.randint(fill_key, (TOK_DEV - MERGED_DEV,), 0, MERGED_DEV, dtype=jnp.int32)
        return jax.random.permutation(order_key, jnp.concatenate([every_slot, further]))
    return jax.vmap(one_block)(block_keys).reshape(TOKENS).astype(jnp.int32)


def touch_ends(values, key, low, largest):
    longest = values.shape.index(max(values.shape))
    spots = []
    for shift in (0, 1):
        where = [jax.random.randint(jax.random.fold_in(key, axis), (), 0, length) for axis, length in enumerate(values.shape)]
        where[longest] = (where[longest] + shift) % values.shape[longest]
        spots.append(tuple(where))
    return values.at[spots[0]].set(low).at[spots[1]].set(largest)


def block_scale(key, shape, pieces, least, top_value):
    def one(position, parts):
        heights = jax.random.uniform(jax.random.fold_in(jax.random.fold_in(key, 6), position), (parts,), jnp.float32, least / len(pieces), top_value / len(pieces))
        return jnp.repeat(jnp.exp(heights), shape[position] // parts).reshape((-1,) + (1,) * (len(shape) - position - 1))

    loudness = one(*pieces[0])
    for cut in pieces[1:]:
        loudness = loudness * one(*cut)
    return loudness


def centred(own_key, shape, width, reach, cuts=(), held_as=jnp.bfloat16):
    loudness = block_scale(own_key, shape, cuts, -0.22, 0.18) if cuts else 1.0
    entries = jax.random.normal(own_key, shape, jnp.float32) * width * loudness
    return jnp.minimum(jnp.maximum(entries, -reach), reach).astype(held_as)


def setup_inputs(seed: int = 0, part: int = 0) -> dict:
    key_list = jax.random.split(jax.random.key(seed), 8)
    part_keys = jax.random.split(jax.random.fold_in(key_list[7], part), 8)
    query_mantissa = draw_query_mantissa(jax.random.fold_in(jax.random.fold_in(key_list[7], part), 71), part)
    key_mantissa = draw_key_mantissa(jax.random.fold_in(jax.random.fold_in(key_list[7], part), 71), part)
    value_mantissa = centred(part_keys[2], (TOKENS, HW), 12.0, 48.0, ((0, 256),))
    query_exponent = touch_ends(jax.random.randint(part_keys[3], (TOKENS, HEADS), -1, 2), jax.random.fold_in(part_keys[3], 1), -1, 1).astype(jnp.int32)
    key_exponent = touch_ends(jax.random.randint(part_keys[4], (TOKENS, HEADS), -1, 2), jax.random.fold_in(part_keys[4], 1), -1, 1).astype(jnp.int32)
    value_exponent = touch_ends(jax.random.randint(part_keys[5], (TOKENS, HEADS), -1, 2), jax.random.fold_in(part_keys[5], 1), -1, 1).astype(jnp.int32)
    merge_map = draw_merge_map(jax.random.fold_in(jax.random.fold_in(key_list[7], part), 71), part)
    return {"query_mantissa": query_mantissa, "key_mantissa": key_mantissa, "value_mantissa": value_mantissa, "query_exponent": query_exponent, "key_exponent": key_exponent, "value_exponent": value_exponent, "merge_map": merge_map}


def sylvester(order_size):
    indices = jnp.arange(order_size, dtype=jnp.int32)
    sign_table = jnp.ones((order_size, order_size), jnp.float32)
    for bit_index in range(order_size.bit_length() - 1):
        bit_value = indices // 2 ** bit_index % 2
        sign_table = sign_table * (1.0 - 2.0 * (bit_value[:, None] * bit_value[None, :]).astype(jnp.float32))
    return sign_table

def rotate(mantissa, exponent, hadamard_table):
    token_count = exponent.shape[0]
    head_count = exponent.shape[1]
    scaling = jnp.exp2(exponent.astype(jnp.float32))
    scaled = (mantissa.astype(jnp.float32).reshape(token_count, head_count, HD) * scaling[:, :, None]).astype(jnp.bfloat16)
    rotated = jnp.dot(scaled.reshape(token_count * head_count, HD), hadamard_table, preferred_element_type=jnp.float32)
    return rotated.reshape(token_count, head_count * HD)

def reference(query_mantissa, key_mantissa, value_mantissa, query_exponent, key_exponent, value_exponent, merge_map):
    inverse_root = 1.0 / math.sqrt(HD)
    hadamard_table = sylvester(HD).astype(jnp.bfloat16)
    queries = (rotate(query_mantissa, query_exponent, hadamard_table) * inverse_root).astype(jnp.bfloat16)
    slot_ids = (jnp.arange(TOKENS, dtype=jnp.int32) // TOK_DEV * MERGED_DEV + merge_map).astype(jnp.int32)
    counts = jax.ops.segment_sum(jnp.ones((TOKENS,), jnp.float32), slot_ids, SLOTS)
    key_sum = jax.ops.segment_sum(rotate(key_mantissa, key_exponent, hadamard_table), slot_ids, SLOTS)
    key_rows = (key_sum / counts[:, None] * inverse_root).astype(jnp.bfloat16)
    value_sum = jax.ops.segment_sum(rotate(value_mantissa, value_exponent, hadamard_table), slot_ids, SLOTS)
    value_rows = (value_sum / counts[:, None] * inverse_root).astype(jnp.bfloat16)
    log_counts = jnp.log(counts)

    def one_head(head_index):
        first_column = (head_index * HD).astype(jnp.int32)
        head_queries = lax.dynamic_slice_in_dim(queries, first_column, HD, 1)
        head_keys = lax.dynamic_slice_in_dim(key_rows, first_column, HD, 1)
        head_values = lax.dynamic_slice_in_dim(value_rows, first_column, HD, 1)
        scores = jnp.dot(head_queries, head_keys.T, preferred_element_type=jnp.float32) * inverse_root + log_counts[None, :]
        row_max = lax.optimization_barrier(jnp.max(scores, axis=1))
        expw = jnp.exp(scores - row_max[:, None])
        denominator = lax.optimization_barrier(jnp.sum(expw, axis=1))
        mixed = jnp.dot(expw.astype(jnp.bfloat16), head_values, preferred_element_type=jnp.float32)
        return (mixed / denominator[:, None]).astype(jnp.bfloat16)
    per_head = lax.map(one_head, jnp.arange(HEADS, dtype=jnp.int32))
    return jnp.transpose(per_head, (1, 0, 2)).reshape(TOKENS, HW)
```

```python
import math

import jax
import jax.numpy as jnp
import numpy as np
from jax import lax
from jax.experimental import pallas as pl
from jax.experimental.pallas import tpu as pltpu
from jax.sharding import Mesh
from jax.sharding import PartitionSpec as P

HD = 128
MERGED = 8
ZH, Y, X, CORE = 4, 8, 4, 2
GROUP = ("zh", "x", "core")
SCALE = 1.0 / math.sqrt(HD)
LOG2E = math.log2(math.e)


def sylvester(size):
    index = np.arange(size)
    both = index[:, None] & index[None, :]
    odd = np.zeros_like(both)
    for bit in range(size.bit_length() - 1):
        odd ^= (both >> bit) & 1
    return (1 - 2 * odd).astype(np.float32)


def prepare_merged_kernel(key_ref, value_ref, key_exp_ref, value_exp_ref, map_ref, table_ref, out_ref, sums):
    tokens = key_ref.shape[0]
    heads = key_exp_ref.shape[1]
    slot = lax.broadcasted_iota(jnp.int32, (MERGED, tokens), 0)
    onehot = (map_ref[...] == slot).astype(jnp.float32)
    counts = jnp.sum(onehot, axis=1, keepdims=True)
    count_rows = jnp.broadcast_to(counts, (MERGED, HD)).astype(jnp.bfloat16)
    for index, (mantissa_ref, exp_ref) in enumerate(((key_ref, key_exp_ref), (value_ref, value_exp_ref))):
        scaling = jnp.exp2(exp_ref[...].astype(jnp.float32)).T
        for head in range(heads):
            chosen = (onehot * scaling[head : head + 1, :]).astype(jnp.bfloat16)
            sums[pl.ds((index * heads + head) * MERGED, MERGED), :] = jnp.dot(
                chosen, mantissa_ref[:, head * HD : (head + 1) * HD], preferred_element_type=jnp.float32
            )
    rotated = jnp.dot(
        sums[...], table_ref[...], precision=lax.Precision.HIGHEST, preferred_element_type=jnp.float32
    ).reshape(2, heads, MERGED, HD)
    merged = (rotated / counts[None, None, :, :] * SCALE).astype(jnp.bfloat16)
    for head in range(heads):
        out_ref[head, 0:MERGED, :] = merged[0, head]
        out_ref[head, MERGED : 2 * MERGED, :] = merged[1, head]
        out_ref[head, 2 * MERGED : 3 * MERGED, :] = count_rows


def prepare_merged(key, value, key_exp, value_exp, merge_map, table):
    heads = key_exp.shape[1]
    return pl.pallas_call(
        prepare_merged_kernel,
        out_shape=jax.ShapeDtypeStruct((heads, 3 * MERGED, HD), jnp.bfloat16),
        scratch_shapes=[pltpu.VMEM((2 * heads * MERGED, HD), jnp.float32)],
        compiler_params=pltpu.CompilerParams(vmem_limit_bytes=24 * 2**20),
        cost_estimate=pl.CostEstimate(flops=2**27, bytes_accessed=2**21, transcendentals=0),
        name="prepare_merged",
    )(key, value, key_exp, value_exp, merge_map.reshape(1, -1), table)


def prepare_queries_kernel(query_ref, exp_ref, table_ref, out_ref):
    heads = exp_ref.shape[1]
    scaling = jnp.exp2(exp_ref[...].astype(jnp.float32)) * SCALE
    for head in range(heads):
        rotated = jnp.dot(
            query_ref[:, head * HD : (head + 1) * HD], table_ref[...], preferred_element_type=jnp.float32
        )
        out_ref[head] = (rotated * scaling[:, head : head + 1]).astype(jnp.bfloat16)


def prepare_queries(query, query_exp, table):
    tokens = query.shape[0]
    heads = query_exp.shape[1]
    return pl.pallas_call(
        prepare_queries_kernel,
        out_shape=jax.ShapeDtypeStruct((heads, tokens, HD), jnp.bfloat16),
        compiler_params=pltpu.CompilerParams(vmem_limit_bytes=16 * 2**20),
        cost_estimate=pl.CostEstimate(flops=2**27, bytes_accessed=2**21, transcendentals=0),
        name="prepare_queries",
    )(query, query_exp, table)


def repack_kernel(in_ref, out_ref):
    sources = in_ref.shape[0]
    half = sources // 2
    rows = half * MERGED
    ones = jnp.full((16, HD), 1.0 / HD, jnp.bfloat16)
    for part in range(2):
        block = in_ref[part * half : (part + 1) * half]
        out_ref[part, 0:rows, :] = block[:, 0:MERGED, :].reshape(rows, HD)
        out_ref[part, rows : 2 * rows, :] = block[:, MERGED : 2 * MERGED, :].reshape(rows, HD)
        spread = block[:, 2 * MERGED : 3 * MERGED, :].reshape(rows, HD)
        counts = lax.dot_general(ones, spread, (((1,), (1,)), ((), ())), preferred_element_type=jnp.float32)
        out_ref[part, 2 * rows : 2 * rows + 16, :] = counts.astype(jnp.bfloat16)


def repack(received):
    sources = received.shape[0]
    rows = sources * MERGED // 2
    return pl.pallas_call(
        repack_kernel,
        out_shape=jax.ShapeDtypeStruct((2, 2 * rows + 16, HD), jnp.bfloat16),
        cost_estimate=pl.CostEstimate(flops=2**20, bytes_accessed=2**18, transcendentals=0),
        name="repack",
    )(received)


def attend_kernel(parts, *refs):
    query_ref = refs[0]
    piece_refs = refs[1 : 1 + parts]
    out_ref, keys, values, logs = refs[1 + parts :]

    @pl.when(pl.program_id(0) == 0)
    def _():
        place = 0
        for piece_ref in piece_refs:
            for half in range(piece_ref.shape[0]):
                rows = HD
                keys[place : place + rows, :] = piece_ref[half, 0:rows, :]
                values[place : place + rows, :] = piece_ref[half, rows : 2 * rows, :]
                counts = piece_ref[half, 2 * rows : 2 * rows + 16, :].astype(jnp.float32)
                logs[:, place : place + rows] = jnp.log(counts[0:8]) * LOG2E
                place += rows

    scores = lax.dot_general(
        query_ref[...], keys[...], (((1,), (1,)), ((), ())), preferred_element_type=jnp.float32
    )
    scores = scores * (SCALE * LOG2E) + logs[0:1, :]
    row_max = jnp.max(scores, axis=1, keepdims=True)
    weights = jnp.exp2(scores - row_max)
    denominator = jnp.sum(weights, axis=1, keepdims=True)
    mixed = jnp.dot(weights.astype(jnp.bfloat16), values[...], preferred_element_type=jnp.float32)
    out_ref[...] = (mixed / denominator).astype(jnp.bfloat16)


def attend(queries, pieces, slots, block=512):
    rows = queries.shape[0]
    parts = len(pieces)
    return pl.pallas_call(
        lambda *refs: attend_kernel(parts, *refs),
        grid=(rows // block,),
        in_specs=[pl.BlockSpec((block, HD), lambda i: (i, 0))]
        + [pl.BlockSpec(piece.shape, lambda i: (0, 0, 0)) for piece in pieces],
        out_specs=pl.BlockSpec((block, HD), lambda i: (i, 0)),
        out_shape=jax.ShapeDtypeStruct((rows, HD), jnp.bfloat16),
        scratch_shapes=[
            pltpu.VMEM((slots, HD), jnp.bfloat16),
            pltpu.VMEM((slots, HD), jnp.bfloat16),
            pltpu.VMEM((8, slots), jnp.float32),
        ],
        compiler_params=pltpu.CompilerParams(vmem_limit_bytes=40 * 2**20),
        cost_estimate=pl.CostEstimate(
            flops=4 * rows * slots * HD, bytes_accessed=4 * rows * HD, transcendentals=rows * slots
        ),
        name="attend",
    )(queries, *pieces)


def unfold_kernel(in_ref, out_ref):
    for head in range(in_ref.shape[0]):
        out_ref[:, head * HD : (head + 1) * HD] = in_ref[head]


def unfold(attended):
    heads, tokens, _ = attended.shape
    return pl.pallas_call(
        unfold_kernel,
        out_shape=jax.ShapeDtypeStruct((tokens, heads * HD), jnp.bfloat16),
        name="unfold",
    )(attended)


def shifted(size, by):
    return [(index, (index + by) % size) for index in range(size)]


def per_device(
    query_mantissa,
    key_mantissa,
    value_mantissa,
    query_exponent,
    key_exponent,
    value_exponent,
    merge_map,
):
    tokens = query_mantissa.shape[0]
    heads = query_exponent.shape[1]
    table = jnp.asarray(sylvester(HD))
    merged = prepare_merged(key_mantissa, value_mantissa, key_exponent, value_exponent, merge_map, table)
    queries = prepare_queries(query_mantissa, query_exponent, table.astype(jnp.bfloat16))
    received = lax.all_to_all(merged, GROUP, split_axis=0, concat_axis=0, tiled=True)
    queries, received = lax.optimization_barrier((queries, received))
    head_queries = lax.all_to_all(queries, GROUP, split_axis=0, concat_axis=0, tiled=True)
    own = repack(received)
    up = down = own
    pieces = [own]
    for step in range(1, Y // 2):
        up = lax.ppermute(up, "y", shifted(Y, 1))
        down = lax.ppermute(down, "y", shifted(Y, -1))
        pieces += [up, down]
    pieces.append(lax.ppermute(up[0:1], "y", shifted(Y, 1)))
    pieces.append(lax.ppermute(down[1:2], "y", shifted(Y, -1)))
    attended = attend(head_queries.reshape(heads * tokens, HD), pieces, Y * heads * MERGED)
    returned = lax.all_to_all(attended.reshape(heads, tokens, HD), GROUP, split_axis=0, concat_axis=0, tiled=True)
    return unfold(returned)


def solution(mesh):
    fine = Mesh(mesh.devices.reshape(ZH, Y, X, CORE, 2), ("zh", "y", "x", "core", "rep"))
    tokens = P(("rep", "zh", "y", "x", "core"), None)
    return jax.shard_map(
        per_device,
        mesh=fine,
        in_specs=(tokens,) * 6 + (P(("rep", "zh", "y", "x", "core")),),
        out_specs=tokens,
        check_vma=False,
    )
```

```python
import math

import jax
import jax.numpy as jnp
import numpy as np
from jax import lax
from jax.experimental import pallas as pl
from jax.experimental.pallas import tpu as pltpu
from jax.sharding import Mesh
from jax.sharding import PartitionSpec as P

HD = 128
MERGED = 8
ZH, Y, X, CORE = 4, 8, 4, 2
GROUP = ("zh", "x", "core")
SCALE = 1.0 / math.sqrt(HD)
LOG2E = math.log2(math.e)


def sylvester(size):
    index = np.arange(size)
    both = index[:, None] & index[None, :]
    odd = np.zeros_like(both)
    for bit in range(size.bit_length() - 1):
        odd ^= (both >> bit) & 1
    return (1 - 2 * odd).astype(np.float32)


def prepare_merged_kernel(
    key_ref, value_ref, key_exp_ref, value_exp_ref, map_ref, table_ref, out_ref, sums, key_held, value_held, arrived
):
    tokens, width = key_held.shape
    heads = width // HD
    chunks = arrived.shape[1]
    piece = width // chunks
    slot = lax.broadcasted_iota(jnp.int32, (MERGED, tokens), 0)
    onehot = (map_ref[...] == slot).astype(jnp.float32)
    counts = jnp.sum(onehot, axis=1, keepdims=True)
    count_rows = jnp.broadcast_to(counts, (MERGED, HD)).astype(jnp.bfloat16)
    sides = ((key_ref, key_held, key_exp_ref), (value_ref, value_held, value_exp_ref))

    def copy(side, chunk):
        columns = pl.ds(chunk * piece, piece)
        return pltpu.make_async_copy(
            sides[side][0].at[:, columns], sides[side][1].at[:, columns], arrived.at[side, chunk]
        )

    for side in range(2):
        for chunk in range(chunks):
            copy(side, chunk).start()
    for side in range(2):
        scaling = jnp.exp2(sides[side][2][...].astype(jnp.float32))
        for head in range(heads):
            if head * HD % piece == 0:
                copy(side, head * HD // piece).wait()
            chosen = (onehot * scaling[head : head + 1, :]).astype(jnp.bfloat16)
            sums[pl.ds((side * heads + head) * MERGED, MERGED), :] = jnp.dot(
                chosen, sides[side][1][:, head * HD : (head + 1) * HD], preferred_element_type=jnp.float32
            )
    rotated = jnp.dot(
        sums[...], table_ref[...], precision=lax.Precision.HIGHEST, preferred_element_type=jnp.float32
    ).reshape(2, heads, MERGED, HD)
    merged = (rotated / counts[None, None, :, :] * SCALE).astype(jnp.bfloat16)
    for head in range(heads):
        out_ref[head, 0:MERGED, :] = merged[0, head]
        out_ref[head, MERGED : 2 * MERGED, :] = merged[1, head]
        out_ref[head, 2 * MERGED : 3 * MERGED, :] = count_rows


def prepare_merged(key, value, key_exp, value_exp, merge_map, table, chunks=4):
    heads = key_exp.shape[0]
    whole = pl.BlockSpec(memory_space=pltpu.VMEM)
    return pl.pallas_call(
        prepare_merged_kernel,
        in_specs=[pl.BlockSpec(memory_space=pl.ANY)] * 2 + [whole] * 4,
        out_specs=whole,
        out_shape=jax.ShapeDtypeStruct((heads, 3 * MERGED, HD), jnp.bfloat16),
        scratch_shapes=[
            pltpu.VMEM((2 * heads * MERGED, HD), jnp.float32),
            pltpu.VMEM(key.shape, jnp.bfloat16),
            pltpu.VMEM(value.shape, jnp.bfloat16),
            pltpu.SemaphoreType.DMA((2, chunks)),
        ],
        compiler_params=pltpu.CompilerParams(vmem_limit_bytes=56 * 2**20),
        cost_estimate=pl.CostEstimate(flops=2**27, bytes_accessed=2**21, transcendentals=0),
        name="prepare_merged",
    )(key, value, key_exp, value_exp, merge_map.reshape(1, -1), table)


def prepare_queries_kernel(query_ref, exp_ref, table_ref, out_ref):
    heads = exp_ref.shape[0]
    scaling = (jnp.exp2(exp_ref[...].astype(jnp.float32)) * SCALE).T
    for head in range(heads):
        rotated = jnp.dot(
            query_ref[:, head * HD : (head + 1) * HD], table_ref[...], preferred_element_type=jnp.float32
        )
        out_ref[head] = (rotated * scaling[:, head : head + 1]).astype(jnp.bfloat16)


def prepare_queries(query, query_exp, table):
    tokens = query.shape[0]
    heads = query_exp.shape[0]
    return pl.pallas_call(
        prepare_queries_kernel,
        out_shape=jax.ShapeDtypeStruct((heads, tokens, HD), jnp.bfloat16),
        compiler_params=pltpu.CompilerParams(vmem_limit_bytes=16 * 2**20),
        cost_estimate=pl.CostEstimate(flops=2**27, bytes_accessed=2**21, transcendentals=0),
        name="prepare_queries",
    )(query, query_exp, table)


def repack_kernel(in_ref, out_ref):
    rows = in_ref.shape[0] * MERGED
    out_ref[0, 0:rows, :] = in_ref[:, 0:MERGED, :].reshape(rows, HD)
    out_ref[0, rows : 2 * rows, :] = in_ref[:, MERGED : 2 * MERGED, :].reshape(rows, HD)
    spread = in_ref[:, 2 * MERGED : 3 * MERGED, :].reshape(rows, HD)
    ones = jnp.full((8, HD), 1.0 / HD, jnp.bfloat16)
    counts = lax.dot_general(ones, spread, (((1,), (1,)), ((), ())), preferred_element_type=jnp.float32)
    out_ref[0, 2 * rows :, :] = jnp.concatenate(
        [counts[:, part * HD : (part + 1) * HD] for part in range(rows // HD)], axis=0
    ).astype(jnp.bfloat16)


def repack(received):
    rows = received.shape[0] * MERGED
    return pl.pallas_call(
        repack_kernel,
        out_shape=jax.ShapeDtypeStruct((1, 2 * rows + 8 * (rows // HD), HD), jnp.bfloat16),
        cost_estimate=pl.CostEstimate(flops=2**20, bytes_accessed=2**18, transcendentals=0),
        name="repack",
    )(received)


def attend_kernel(parts, sub, *refs):
    query_ref = refs[0]
    piece_refs = refs[1 : 1 + parts]
    out_ref, keys, values, logs = refs[1 + parts :]

    @pl.when(pl.program_id(0) == 0)
    def _():
        place = 0
        rows = 2 * HD
        for piece_ref in piece_refs:
            for block in range(piece_ref.shape[0]):
                keys[place : place + rows, :] = piece_ref[block, 0:rows, :]
                values[place : place + rows, 0:HD] = piece_ref[block, rows : 2 * rows, :]
                counts = piece_ref[block, 2 * rows : 2 * rows + 16, :].astype(jnp.float32)
                logs[:, place : place + HD] = jnp.log(counts[0:8]) * LOG2E
                logs[:, place + HD : place + rows] = jnp.log(counts[8:16]) * LOG2E
                place += rows
        values[:, HD:] = jnp.ones((place, HD), jnp.bfloat16)

    for start in range(0, query_ref.shape[0], sub):
        scores = lax.dot_general(
            query_ref[start : start + sub, :],
            keys[...],
            (((1,), (1,)), ((), ())),
            preferred_element_type=jnp.float32,
        )
        scores = scores * (SCALE * LOG2E) + logs[0:1, :]
        weights = jnp.exp2(scores - jnp.max(scores, axis=1, keepdims=True)).astype(jnp.bfloat16)
        mixed = jnp.dot(weights, values[...], preferred_element_type=jnp.float32)
        out_ref[start : start + sub, :] = (mixed[:, 0:HD] / mixed[:, HD:]).astype(jnp.bfloat16)


def attend(queries, pieces, slots, block=2048, sub=256):
    rows = queries.shape[0]
    parts = len(pieces)
    return pl.pallas_call(
        lambda *refs: attend_kernel(parts, sub, *refs),
        grid=(rows // block,),
        in_specs=[pl.BlockSpec((block, HD), lambda i: (i, 0))]
        + [pl.BlockSpec(piece.shape, lambda i: (0, 0, 0)) for piece in pieces],
        out_specs=pl.BlockSpec((block, HD), lambda i: (i, 0)),
        out_shape=jax.ShapeDtypeStruct((rows, HD), jnp.bfloat16),
        scratch_shapes=[
            pltpu.VMEM((slots, HD), jnp.bfloat16),
            pltpu.VMEM((slots, 2 * HD), jnp.bfloat16),
            pltpu.VMEM((8, slots), jnp.float32),
        ],
        compiler_params=pltpu.CompilerParams(vmem_limit_bytes=56 * 2**20),
        cost_estimate=pl.CostEstimate(
            flops=4 * rows * slots * HD, bytes_accessed=4 * rows * HD, transcendentals=rows * slots
        ),
        name="attend",
    )(queries, *pieces)


def unfold_kernel(in_ref, out_ref):
    for head in range(in_ref.shape[0]):
        out_ref[:, head * HD : (head + 1) * HD] = in_ref[head]


def unfold(attended, steps=4):
    heads, tokens, _ = attended.shape
    group = heads // steps
    return pl.pallas_call(
        unfold_kernel,
        grid=(steps,),
        in_specs=[pl.BlockSpec((group, tokens, HD), lambda i: (i, 0, 0))],
        out_specs=pl.BlockSpec((tokens, group * HD), lambda i: (0, i)),
        out_shape=jax.ShapeDtypeStruct((tokens, heads * HD), jnp.bfloat16),
        name="unfold",
    )(attended)


def shifted(size, by):
    return [(index, (index + by) % size) for index in range(size)]


def per_device(
    query_mantissa,
    key_mantissa,
    value_mantissa,
    query_exponent,
    key_exponent,
    value_exponent,
    merge_map,
):
    tokens = query_mantissa.shape[0]
    heads = query_exponent.shape[1]
    table = jnp.asarray(sylvester(HD))
    merged = prepare_merged(key_mantissa, value_mantissa, key_exponent.T, value_exponent.T, merge_map, table)
    merged, query_mantissa = lax.optimization_barrier((merged, query_mantissa))
    queries = prepare_queries(query_mantissa, query_exponent.T, table.astype(jnp.bfloat16))
    received = lax.all_to_all(merged, GROUP, split_axis=0, concat_axis=0, tiled=True)
    head_queries = lax.all_to_all(queries, GROUP, split_axis=0, concat_axis=0, tiled=True)
    same = lax.all_gather(repack(received), "yA", axis=0, tiled=True)
    up = lax.ppermute(same[0:2], ("yA", "yB"), shifted(Y, 1))
    down = lax.ppermute(same[2:4], ("yA", "yB"), shifted(Y, -1))
    attended = attend(head_queries.reshape(heads * tokens, HD), (same, up, down), Y * heads * MERGED)
    returned = lax.all_to_all(attended.reshape(heads, tokens, HD), GROUP, split_axis=0, concat_axis=0, tiled=True)
    return unfold(returned)


def solution(mesh):
    fine = Mesh(mesh.devices.reshape(ZH, Y // 2, 2, X, CORE, 2), ("zh", "yA", "yB", "x", "core", "rep"))
    tokens = P(("rep", "zh", "yA", "yB", "x", "core"), None)
    return jax.shard_map(
        per_device,
        mesh=fine,
        in_specs=(tokens,) * 6 + (P(("rep", "zh", "yA", "yB", "x", "core")),),
        out_specs=tokens,
        check_vma=False,
    )
```

```python
import math

import jax
import jax.numpy as jnp
import numpy as np
from jax import lax
from jax.experimental import pallas as pl
from jax.experimental.pallas import tpu as pltpu
from jax.sharding import Mesh
from jax.sharding import PartitionSpec as P

HD = 128
MERGED = 8
ZH, Y, X, CORE = 4, 8, 4, 2
GROUP = ("yB", "x", "core")
RING = ("zh", "yA", "core")
SCALE = 1.0 / math.sqrt(HD)
LOG2E = math.log2(math.e)


def sylvester(size):
    index = np.arange(size)
    both = index[:, None] & index[None, :]
    odd = np.zeros_like(both)
    for bit in range(size.bit_length() - 1):
        odd ^= (both >> bit) & 1
    return (1 - 2 * odd).astype(np.float32)


def prepare_merged_kernel(
    key_ref, value_ref, key_exp_ref, value_exp_ref, map_ref, table_ref, out_ref, sums, key_held, value_held, arrived
):
    tokens, width = key_held.shape
    heads = width // HD
    chunks = arrived.shape[1]
    piece = width // chunks
    slot = lax.broadcasted_iota(jnp.int32, (MERGED, tokens), 0)
    onehot = (map_ref[...] == slot).astype(jnp.float32)
    counts = jnp.sum(onehot, axis=1, keepdims=True)
    count_rows = jnp.broadcast_to(counts, (MERGED, HD)).astype(jnp.bfloat16)
    sides = ((key_ref, key_held, key_exp_ref), (value_ref, value_held, value_exp_ref))

    def copy(side, chunk):
        columns = pl.ds(chunk * piece, piece)
        return pltpu.make_async_copy(
            sides[side][0].at[:, columns], sides[side][1].at[:, columns], arrived.at[side, chunk]
        )

    for side in range(2):
        for chunk in range(chunks):
            copy(side, chunk).start()
    for side in range(2):
        scaling = jnp.exp2(sides[side][2][...].astype(jnp.float32))
        for head in range(heads):
            if head * HD % piece == 0:
                copy(side, head * HD // piece).wait()
            chosen = (onehot * scaling[head : head + 1, :]).astype(jnp.bfloat16)
            sums[pl.ds((side * heads + head) * MERGED, MERGED), :] = jnp.dot(
                chosen, sides[side][1][:, head * HD : (head + 1) * HD], preferred_element_type=jnp.float32
            )
    rotated = jnp.dot(
        sums[...], table_ref[...], precision=lax.Precision.HIGHEST, preferred_element_type=jnp.float32
    ).reshape(2, heads, MERGED, HD)
    merged = (rotated / counts[None, None, :, :] * SCALE).astype(jnp.bfloat16)
    pair = out_ref.shape[1] // (2 * MERGED)
    for head in range(heads):
        target, place = head // pair, head % pair * 2 * MERGED
        out_ref[target, place : place + MERGED, :] = merged[0, head]
        out_ref[target, place + MERGED : place + 2 * MERGED, :] = merged[1, head]
    for target in range(heads // pair):
        out_ref[target, pair * 2 * MERGED :, :] = count_rows


def prepare_merged(key, value, key_exp, value_exp, merge_map, table, targets, chunks=4):
    heads = key_exp.shape[0]
    rows = heads // targets * 2 * MERGED + MERGED
    whole = pl.BlockSpec(memory_space=pltpu.VMEM)
    return pl.pallas_call(
        prepare_merged_kernel,
        in_specs=[pl.BlockSpec(memory_space=pl.ANY)] * 2 + [whole] * 4,
        out_specs=whole,
        out_shape=jax.ShapeDtypeStruct((targets, rows, HD), jnp.bfloat16),
        scratch_shapes=[
            pltpu.VMEM((2 * heads * MERGED, HD), jnp.float32),
            pltpu.VMEM(key.shape, jnp.bfloat16),
            pltpu.VMEM(value.shape, jnp.bfloat16),
            pltpu.SemaphoreType.DMA((2, chunks)),
        ],
        compiler_params=pltpu.CompilerParams(vmem_limit_bytes=56 * 2**20),
        cost_estimate=pl.CostEstimate(flops=2**27, bytes_accessed=2**21, transcendentals=0),
        name="prepare_merged",
    )(key, value, key_exp, value_exp, merge_map.reshape(1, -1), table)


def prepare_queries_kernel(query_ref, exp_ref, table_ref, out_ref):
    heads = exp_ref.shape[0]
    scaling = (jnp.exp2(exp_ref[...].astype(jnp.float32)) * SCALE).T
    for head in range(heads):
        rotated = jnp.dot(
            query_ref[:, head * HD : (head + 1) * HD], table_ref[...], preferred_element_type=jnp.float32
        )
        out_ref[head] = (rotated * scaling[:, head : head + 1]).astype(jnp.bfloat16)


def prepare_queries(query, query_exp, table):
    tokens = query.shape[0]
    heads = query_exp.shape[0]
    return pl.pallas_call(
        prepare_queries_kernel,
        out_shape=jax.ShapeDtypeStruct((heads, tokens, HD), jnp.bfloat16),
        compiler_params=pltpu.CompilerParams(vmem_limit_bytes=16 * 2**20),
        cost_estimate=pl.CostEstimate(flops=2**27, bytes_accessed=2**21, transcendentals=0),
        name="prepare_queries",
    )(query, query_exp, table)


def repack_kernel(in_ref, out_ref):
    sources, height, _ = in_ref.shape
    rows = sources * MERGED
    for kind in range(height // MERGED - 1):
        out_ref[0, kind * rows : (kind + 1) * rows, :] = in_ref[
            :, kind * MERGED : (kind + 1) * MERGED, :
        ].reshape(rows, HD)
    spread = in_ref[:, height - MERGED :, :].reshape(rows, HD)
    ones = jnp.full((16, HD), 1.0 / HD, jnp.bfloat16)
    counts = lax.dot_general(ones, spread, (((1,), (1,)), ((), ())), preferred_element_type=jnp.float32)
    out_ref[0, (height // MERGED - 1) * rows :, :] = counts.astype(jnp.bfloat16)


def repack(received):
    sources, height, _ = received.shape
    rows = sources * MERGED
    return pl.pallas_call(
        repack_kernel,
        out_shape=jax.ShapeDtypeStruct((1, (height // MERGED - 1) * rows + 16, HD), jnp.bfloat16),
        cost_estimate=pl.CostEstimate(flops=2**20, bytes_accessed=2**18, transcendentals=0),
        name="repack",
    )(received)


def attend_kernel(parts, first, last, sub, *refs):
    query_ref = refs[0]
    piece_refs = refs[1 : 1 + parts]
    refs = refs[1 + parts :]
    if not first:
        mixed_ref, aside_ref = refs[:2]
        refs = refs[2:]
    out_refs = refs[: 1 if last else 2]
    keys, values, logs = refs[1 if last else 2 :]
    tokens = query_ref.shape[1]
    step = sub // tokens

    @pl.when(pl.program_id(1) == 0)
    def _():
        base = pl.multiple_of(pl.program_id(0) * 2 * HD, 2 * HD)
        place = 0
        for piece_ref in piece_refs:
            for block in range(piece_ref.shape[0]):
                keys[place : place + HD, :] = piece_ref[block, pl.ds(base, HD), :]
                values[place : place + HD, 0:HD] = piece_ref[block, pl.ds(base + HD, HD), :]
                counts = piece_ref[block, 4 * HD : 4 * HD + 16, :].astype(jnp.float32)
                logs[:, place : place + HD] = jnp.log(counts[0:8]) * LOG2E
                place += HD
        values[:, HD:] = jnp.ones((place, HD), jnp.bfloat16)

    lower = lax.broadcasted_iota(jnp.int32, (sub, HD), 1) < HD // 2
    for index in range(query_ref.shape[0] // step):
        rows = slice(index * sub, (index + 1) * sub)
        scores = lax.dot_general(
            query_ref[index * step : (index + 1) * step].reshape(sub, HD),
            keys[...],
            (((1,), (1,)), ((), ())),
            preferred_element_type=jnp.float32,
        )
        scores = scores * (SCALE * LOG2E) + logs[0:1, :]
        top = jnp.max(scores, axis=1, keepdims=True)
        if not first:
            before = aside_ref[rows, 0:1]
            top = jnp.maximum(top, before)
        weights = jnp.exp2(scores - top).astype(jnp.bfloat16)
        both = jnp.dot(weights, values[...], preferred_element_type=jnp.float32)
        mixed = both[:, 0:HD]
        denominator = both[:, HD:]
        if not first:
            rescale = jnp.exp2(before - top)
            mixed = mixed + mixed_ref[rows, :] * rescale
            denominator = denominator + aside_ref[rows, HD - 1 : HD] * rescale
        if last:
            done = (mixed / denominator).astype(jnp.bfloat16)
            out_refs[0][index * step : (index + 1) * step] = done.reshape(step, tokens, HD)
        else:
            out_refs[0][rows, :] = mixed
            out_refs[1][rows, :] = jnp.where(lower, top, denominator)


def attend(queries, pieces, state, last, sub=256, cuts=2):
    sources, pair, tokens, _ = queries.shape
    rows = sources * tokens // cuts
    parts = len(pieces)
    slots = HD * sum(piece.shape[0] for piece in pieces)
    first = state is None
    by_head = pl.BlockSpec((sources // cuts, None, tokens, HD), lambda head, cut: (cut, head, 0, 0))
    state_specs = [pl.BlockSpec((None, rows, HD), lambda head, cut: (head, cut, 0))] * 2
    if last:
        out_specs = by_head
        out_shape = jax.ShapeDtypeStruct(queries.shape, jnp.bfloat16)
    else:
        out_specs = state_specs
        out_shape = [jax.ShapeDtypeStruct((pair, sources * tokens, HD), jnp.float32)] * 2
    return pl.pallas_call(
        lambda *refs: attend_kernel(parts, first, last, sub, *refs),
        grid=(pair, cuts),
        in_specs=[by_head]
        + [pl.BlockSpec(piece.shape, lambda head, cut: (0, 0, 0)) for piece in pieces]
        + ([] if first else state_specs),
        out_specs=out_specs,
        out_shape=out_shape,
        scratch_shapes=[
            pltpu.VMEM((slots, HD), jnp.bfloat16),
            pltpu.VMEM((slots, 2 * HD), jnp.bfloat16),
            pltpu.VMEM((8, slots), jnp.float32),
        ],
        compiler_params=pltpu.CompilerParams(vmem_limit_bytes=24 * 2**20),
        cost_estimate=pl.CostEstimate(
            flops=8 * pair * cuts * rows * slots * HD,
            bytes_accessed=16 * pair * cuts * rows * HD,
            transcendentals=pair * cuts * rows * slots,
        ),
        name="attend",
    )(queries, *pieces, *(() if first else state))


def place(zh, ya, core):
    return (zh % ZH * (Y // 2) + ya % (Y // 2)) * CORE + core


def first_groups():
    over_z = [[place(zh, ya, 0) for zh in range(ZH)] for ya in range(Y // 2)]
    over_y = [[place(zh, ya, 1) for ya in range(Y // 2)] for zh in range(ZH)]
    return over_z + over_y


def second_ring(by):
    pairs = []
    for zh in range(ZH):
        for ya in range(Y // 2):
            pairs.append((place(zh, ya, 0), place(zh, ya + by, 0)))
            pairs.append((place(zh, ya, 1), place(zh + by, ya, 1)))
    return pairs


def per_device(
    query_mantissa,
    key_mantissa,
    value_mantissa,
    query_exponent,
    key_exponent,
    value_exponent,
    merge_map,
):
    tokens = query_mantissa.shape[0]
    heads = query_exponent.shape[1]
    table = jnp.asarray(sylvester(HD))
    targets = lax.axis_size(GROUP)
    merged = prepare_merged(
        key_mantissa, value_mantissa, key_exponent.T, value_exponent.T, merge_map, table, targets
    )
    queries = prepare_queries(query_mantissa, query_exponent.T, table.astype(jnp.bfloat16))
    received = lax.all_to_all(merged, GROUP, split_axis=0, concat_axis=0, tiled=True)
    head_queries = lax.all_to_all(queries, GROUP, split_axis=0, concat_axis=0, tiled=True)
    head_queries = head_queries.reshape(targets, heads // targets, tokens, HD)
    near = lax.all_gather(repack(received), RING, axis=0, tiled=True, axis_index_groups=first_groups())
    up = lax.ppermute(near, RING, second_ring(1))
    down = lax.ppermute(near, RING, second_ring(-1))
    state = attend(head_queries, (near,), None, False)
    up, down, state = lax.optimization_barrier((up, down, state))
    far_up = lax.ppermute(up[0:2], RING, second_ring(1))
    far_down = lax.ppermute(down[2:4], RING, second_ring(-1))
    state = attend(head_queries, (up, down), state, False)
    attended = attend(head_queries, (far_up, far_down), state, True)
    returned = lax.all_to_all(
        attended.reshape(heads, tokens, HD), GROUP, split_axis=0, concat_axis=0, tiled=True
    )
    return jnp.transpose(returned, (1, 0, 2)).reshape(tokens, heads * HD)


def solution(mesh):
    fine = Mesh(mesh.devices.reshape(ZH, Y // 2, 2, X, CORE, 2), ("zh", "yA", "yB", "x", "core", "rep"))
    tokens = P(("rep", "zh", "yA", "yB", "x", "core"), None)
    return jax.shard_map(
        per_device,
        mesh=fine,
        in_specs=(tokens,) * 6 + (P(("rep", "zh", "yA", "yB", "x", "core")),),
        out_specs=tokens,
        check_vma=False,
    )
```

```python
import math

import jax
import jax.numpy as jnp
import numpy as np
from jax import lax
from jax.experimental import pallas as pl
from jax.experimental.pallas import tpu as pltpu
from jax.sharding import Mesh
from jax.sharding import PartitionSpec as P

HD = 128
MERGED = 8
ZH, Y, X, CORE = 4, 8, 4, 2
GROUP = ("yB", "x", "core")
RING = ("zh", "yA", "yB", "core", "rep")
REP = 2
SCALE = 1.0 / math.sqrt(HD)
LOG2E = math.log2(math.e)


def sylvester():
    row = lax.broadcasted_iota(jnp.int32, (HD, HD), 0)
    column = lax.broadcasted_iota(jnp.int32, (HD, HD), 1)
    both = row & column
    odd = both
    for bit in range(1, HD.bit_length() - 1):
        odd = odd ^ (both >> bit)
    return (1 - 2 * (odd & 1)).astype(jnp.float32)


def columns_of(source, held, arrived, chunks):
    piece = held.shape[1] // chunks
    copies = []
    for chunk in range(chunks):
        columns = pl.ds(chunk * piece, piece)
        copies.append(pltpu.make_async_copy(source.at[:, columns], held.at[:, columns], arrived.at[chunk]))
    return copies


def prepare_merged_kernel(
    chunks, key_ref, value_ref, key_exp_ref, value_exp_ref, map_ref, out_ref, sums, held, exps, where, arrived, small
):
    tokens, width = held.shape[1:]
    heads = width // HD
    exponents = [
        pltpu.make_async_copy(key_exp_ref, exps.at[0], small.at[0]),
        pltpu.make_async_copy(value_exp_ref, exps.at[1], small.at[1]),
    ]
    mapped = pltpu.make_async_copy(map_ref, where, small.at[2])
    sides = [
        columns_of(source, held.at[side], arrived.at[side], chunks)
        for side, source in enumerate((key_ref, value_ref))
    ]
    mapped.start()
    exponents[0].start()
    for copy in sides[0]:
        copy.start()
    exponents[1].start()
    for copy in sides[1]:
        copy.start()
    table = sylvester()
    mapped.wait()
    slot = lax.broadcasted_iota(jnp.int32, (MERGED, tokens), 0)
    onehot = (where[...] == slot).astype(jnp.float32)
    counts = jnp.sum(onehot, axis=1, keepdims=True)
    spread = jnp.where(
        lax.broadcasted_iota(jnp.int32, (MERGED, HD), 1)
        == lax.broadcasted_iota(jnp.int32, (MERGED, HD), 0) + MERGED * lax.axis_index(GROUP),
        counts,
        0.0,
    )
    count_rows = jnp.broadcast_to(jnp.sum(spread, axis=0, keepdims=True), (MERGED, HD)).astype(jnp.bfloat16)
    for side in range(2):
        exponents[side].wait()
        scaling = jnp.exp2(exps[side].astype(jnp.float32))
        for head in range(heads):
            if head * chunks % heads == 0:
                sides[side][head * chunks // heads].wait()
            chosen = (onehot * scaling[head : head + 1, :]).astype(jnp.bfloat16)
            start = (side * heads + head) * MERGED
            sums[start : start + MERGED, :] = jnp.dot(
                chosen, held[side, :, head * HD : (head + 1) * HD], preferred_element_type=jnp.float32
            )
    rotated = jnp.dot(
        sums[...], table, precision=lax.Precision.HIGHEST, preferred_element_type=jnp.float32
    ).reshape(2, heads, MERGED, HD)
    merged = (rotated / counts[None, None, :, :] * SCALE).astype(jnp.bfloat16)
    pair = out_ref.shape[1] // (2 * MERGED)
    for head in range(heads):
        target, place = head // pair, head % pair * 2 * MERGED
        out_ref[target, place : place + MERGED, :] = merged[0, head]
        out_ref[target, place + MERGED : place + 2 * MERGED, :] = merged[1, head]
    for target in range(heads // pair):
        out_ref[target, pair * 2 * MERGED :, :] = count_rows


def prepare_merged(key, value, key_exp, value_exp, merge_map, targets, chunks=2):
    heads = key_exp.shape[0]
    rows = heads // targets * 2 * MERGED + MERGED
    merge_map = merge_map.reshape(1, -1)
    return pl.pallas_call(
        lambda *refs: prepare_merged_kernel(chunks, *refs),
        in_specs=[pl.BlockSpec(memory_space=pl.ANY)] * 5,
        out_specs=pl.BlockSpec(memory_space=pltpu.VMEM),
        out_shape=jax.ShapeDtypeStruct((targets, rows, HD), jnp.bfloat16),
        scratch_shapes=[
            pltpu.VMEM((2 * heads * MERGED, HD), jnp.float32),
            pltpu.VMEM((2, *key.shape), jnp.bfloat16),
            pltpu.VMEM((2, *key_exp.shape), jnp.int32),
            pltpu.VMEM(merge_map.shape, jnp.int32),
            pltpu.SemaphoreType.DMA((2, chunks)),
            pltpu.SemaphoreType.DMA((3,)),
        ],
        compiler_params=pltpu.CompilerParams(vmem_limit_bytes=56 * 2**20),
        cost_estimate=pl.CostEstimate(flops=2**27, bytes_accessed=2**21, transcendentals=0),
        name="prepare_merged",
    )(key, value, key_exp, value_exp, merge_map)


def prepare_queries_kernel(chunks, query_ref, exp_ref, out_ref, held, exps, arrived, small):
    heads = exps.shape[0]
    exponents = pltpu.make_async_copy(exp_ref, exps, small.at[0])
    copies = columns_of(query_ref, held, arrived, chunks)
    exponents.start()
    for copy in copies:
        copy.start()
    table = sylvester().astype(jnp.bfloat16)
    exponents.wait()
    scaling = (jnp.exp2(exps[...].astype(jnp.float32)) * SCALE).T
    for head in range(heads):
        if head * chunks % heads == 0:
            copies[head * chunks // heads].wait()
        rotated = jnp.dot(
            held[:, head * HD : (head + 1) * HD], table, preferred_element_type=jnp.float32
        )
        out_ref[head] = (rotated * scaling[:, head : head + 1]).astype(jnp.bfloat16)


def prepare_queries(query, query_exp, chunks=2):
    tokens = query.shape[0]
    heads = query_exp.shape[0]
    return pl.pallas_call(
        lambda *refs: prepare_queries_kernel(chunks, *refs),
        in_specs=[pl.BlockSpec(memory_space=pl.ANY)] * 2,
        out_specs=pl.BlockSpec(memory_space=pltpu.VMEM),
        out_shape=jax.ShapeDtypeStruct((heads, tokens, HD), jnp.bfloat16),
        scratch_shapes=[
            pltpu.VMEM(query.shape, jnp.bfloat16),
            pltpu.VMEM(query_exp.shape, jnp.int32),
            pltpu.SemaphoreType.DMA((chunks,)),
            pltpu.SemaphoreType.DMA((1,)),
        ],
        compiler_params=pltpu.CompilerParams(vmem_limit_bytes=56 * 2**20),
        cost_estimate=pl.CostEstimate(flops=2**27, bytes_accessed=2**21, transcendentals=0),
        name="prepare_queries",
    )(query, query_exp)


def repack_kernel(in_ref, out_ref):
    sources, height, _ = in_ref.shape
    rows = sources * MERGED
    for kind in range(height // MERGED - 1):
        out_ref[0, kind * rows : (kind + 1) * rows, :] = in_ref[
            :, kind * MERGED : (kind + 1) * MERGED, :
        ].reshape(rows, HD)
    counts = jnp.sum(in_ref[:, height - MERGED :, :].astype(jnp.float32), axis=0)
    out_ref[0, (height // MERGED - 1) * rows :, :] = jnp.concatenate([counts] * 2, axis=0).astype(jnp.bfloat16)


def repack(received):
    sources, height, _ = received.shape
    rows = sources * MERGED
    return pl.pallas_call(
        repack_kernel,
        out_shape=jax.ShapeDtypeStruct((1, (height // MERGED - 1) * rows + 16, HD), jnp.bfloat16),
        cost_estimate=pl.CostEstimate(flops=2**20, bytes_accessed=2**18, transcendentals=0),
        name="repack",
    )(received)


def attend_kernel(parts, first, last, sub, *refs):
    query_ref = refs[0]
    piece_refs = refs[1 : 1 + parts]
    refs = refs[1 + parts :]
    if not first:
        both_ref, top_ref = refs[:2]
        refs = refs[2:]
    out_refs = refs[: 1 if last else 2]
    keys, values, logs = refs[1 if last else 2 :]
    sources, pair, tokens, _ = query_ref.shape
    step = sub // tokens
    place = 0
    for piece_ref in piece_refs:
        for block in range(piece_ref.shape[0]):
            for head in range(pair):
                base = head * 2 * HD
                keys[head, place : place + HD, :] = piece_ref[block, base : base + HD, :]
                values[head, place : place + HD, 0:HD] = piece_ref[block, base + HD : base + 2 * HD, :]
            counts = piece_ref[block, 2 * pair * HD : 2 * pair * HD + 16, :].astype(jnp.float32)
            logs[:, place : place + HD] = jnp.log(counts[0:8]) * LOG2E
            place += HD
    values[:, :, HD:] = jnp.ones((pair, place, HD), jnp.bfloat16)

    def score(head, index):
        scores = lax.dot_general(
            query_ref[index * step : (index + 1) * step, head].reshape(sub, HD),
            keys[head],
            (((1,), (1,)), ((), ())),
            preferred_element_type=jnp.float32,
        )
        return scores * (SCALE * LOG2E) + logs[0:1, :]

    def mix(head, index, scores):
        rows = slice(index * sub, (index + 1) * sub)
        top = jnp.broadcast_to(jnp.max(scores, axis=1, keepdims=True), (sub, HD))
        if not first:
            before = top_ref[head, rows, :]
            top = jnp.maximum(top, before)
            rescale = jnp.exp2(before - top)
        weights = jnp.exp2(scores - jnp.concatenate([top] * (place // HD), axis=1)).astype(jnp.bfloat16)
        both = jnp.dot(weights, values[head], preferred_element_type=jnp.float32)
        if not first:
            both = both + both_ref[head, rows, :] * jnp.concatenate([rescale] * 2, axis=1)
        if last:
            done = (both[:, 0:HD] / both[:, HD:]).astype(jnp.bfloat16)
            out_refs[0][index * step : (index + 1) * step, head] = done.reshape(step, tokens, HD)
        else:
            out_refs[0][head, rows, :] = both
            out_refs[1][head, rows, :] = top

    tiles = [(head, index) for head in range(pair) for index in range(sources // step)]
    upcoming = score(*tiles[0])
    for number, tile in enumerate(tiles):
        scores = upcoming
        if number + 1 < len(tiles):
            upcoming = score(*tiles[number + 1])
        mix(*tile, scores)


def attend(queries, pieces, state, last, sub=256):
    sources, pair, tokens, _ = queries.shape
    rows = sources * tokens
    parts = len(pieces)
    slots = HD * sum(piece.shape[0] for piece in pieces)
    first = state is None
    if last:
        out_shape = jax.ShapeDtypeStruct(queries.shape, jnp.bfloat16)
    else:
        out_shape = [jax.ShapeDtypeStruct((pair, rows, width), jnp.float32) for width in (2 * HD, HD)]
    return pl.pallas_call(
        lambda *refs: attend_kernel(parts, first, last, sub, *refs),
        out_shape=out_shape,
        scratch_shapes=[
            pltpu.VMEM((pair, slots, HD), jnp.bfloat16),
            pltpu.VMEM((pair, slots, 2 * HD), jnp.bfloat16),
            pltpu.VMEM((8, slots), jnp.float32),
        ],
        compiler_params=pltpu.CompilerParams(vmem_limit_bytes=24 * 2**20),
        cost_estimate=pl.CostEstimate(
            flops=8 * pair * rows * slots * HD,
            bytes_accessed=16 * pair * rows * HD,
            transcendentals=pair * rows * slots,
        ),
        name="attend",
    )(queries, *pieces, *(() if first else state))


def place(zh, ya, yb, core, rep):
    return (((zh % ZH * (Y // 2) + ya % (Y // 2)) * 2 + yb) * CORE + core) * REP + rep


def ring(by, over_y):
    pairs = []
    for zh, ya, yb, core, rep in np.ndindex(ZH, Y // 2, 2, CORE, REP):
        if core == over_y:
            moved = (zh, ya + (by if yb == 0 else -by))
        else:
            moved = (zh + (by if rep == 0 else -by), ya)
        pairs.append((place(zh, ya, yb, core, rep), place(*moved, yb, core, rep)))
    return pairs


def first_ring(by):
    return ring(by, 1)


def second_ring(by):
    return ring(by, 0)


def per_device(
    query_mantissa,
    key_mantissa,
    value_mantissa,
    query_exponent,
    key_exponent,
    value_exponent,
    merge_map,
):
    tokens = query_mantissa.shape[0]
    heads = query_exponent.shape[1]
    targets = lax.axis_size(GROUP)
    merged = prepare_merged(key_mantissa, value_mantissa, key_exponent.T, value_exponent.T, merge_map, targets)
    queries = prepare_queries(query_mantissa, query_exponent.T)
    received = lax.all_to_all(merged, GROUP, split_axis=0, concat_axis=0, tiled=True)
    received, queries = lax.optimization_barrier((received, queries))
    own = repack(received)
    queries, own = lax.optimization_barrier((queries, own))
    head_queries = lax.all_to_all(queries, GROUP, split_axis=0, concat_axis=0, tiled=True)
    head_queries = head_queries.reshape(targets, heads // targets, tokens, HD)
    near = jnp.concatenate([own] + [lax.ppermute(own, RING, first_ring(by)) for by in (1, -1, 2)], axis=0)
    up = lax.ppermute(near, RING, second_ring(1))
    down = lax.ppermute(near, RING, second_ring(-1))
    state = attend(head_queries, (near,), None, False)
    up, state = lax.optimization_barrier((up, state))
    far = lax.ppermute(up, RING, second_ring(1))
    state = attend(head_queries, (up, down), state, False)
    attended = attend(head_queries, (far,), state, True)
    returned = lax.all_to_all(
        attended.reshape(heads, tokens, HD), GROUP, split_axis=0, concat_axis=0, tiled=True
    )
    return jnp.transpose(returned, (1, 0, 2)).reshape(tokens, heads * HD)


def solution(mesh):
    fine = Mesh(mesh.devices.reshape(ZH, Y // 2, 2, X, CORE, 2), ("zh", "yA", "yB", "x", "core", "rep"))
    tokens = P(("rep", "zh", "yA", "yB", "x", "core"), None)
    return jax.shard_map(
        per_device,
        mesh=fine,
        in_specs=(tokens,) * 6 + (P(("rep", "zh", "yA", "yB", "x", "core")),),
        out_specs=tokens,
        check_vma=False,
    )
```

```python
import math

import jax
import jax.numpy as jnp
import numpy as np
from jax import lax
from jax.experimental import pallas as pl
from jax.experimental.pallas import tpu as pltpu
from jax.sharding import Mesh
from jax.sharding import PartitionSpec as P

HD = 128
MERGED = 8
ZH, Y, X, CORE = 4, 8, 4, 2
GROUP = ("yB", "x", "core")
RING = ("zh", "yA", "yB", "core", "rep")
REP = 2
SCALE = 1.0 / math.sqrt(HD)
LOG2E = math.log2(math.e)


def sylvester():
    row = lax.broadcasted_iota(jnp.int32, (HD, HD), 0)
    column = lax.broadcasted_iota(jnp.int32, (HD, HD), 1)
    both = row & column
    odd = both
    for bit in range(1, HD.bit_length() - 1):
        odd = odd ^ (both >> bit)
    return (1 - 2 * (odd & 1)).astype(jnp.float32)


def columns_of(source, held, arrived, chunks):
    piece = held.shape[1] // chunks
    copies = []
    for chunk in range(chunks):
        columns = pl.ds(chunk * piece, piece)
        copies.append(pltpu.make_async_copy(source.at[:, columns], held.at[:, columns], arrived.at[chunk]))
    return copies


def prepare_merged_kernel(
    chunks, key_ref, value_ref, key_exp_ref, value_exp_ref, map_ref, out_ref, sums, held, exps, where, arrived, small
):
    tokens, width = held.shape[1:]
    heads = width // HD
    exponents = [
        pltpu.make_async_copy(key_exp_ref, exps.at[0], small.at[0]),
        pltpu.make_async_copy(value_exp_ref, exps.at[1], small.at[1]),
    ]
    mapped = pltpu.make_async_copy(map_ref, where, small.at[2])
    sides = [
        columns_of(source, held.at[side], arrived.at[side], chunks)
        for side, source in enumerate((key_ref, value_ref))
    ]
    mapped.start()
    exponents[0].start()
    for copy in sides[0]:
        copy.start()
    exponents[1].start()
    for copy in sides[1]:
        copy.start()
    table = sylvester()
    mapped.wait()
    slot = lax.broadcasted_iota(jnp.int32, (MERGED, tokens), 0)
    onehot = (where[...] == slot).astype(jnp.float32)
    counts = jnp.sum(onehot, axis=1, keepdims=True)
    spread = jnp.where(
        lax.broadcasted_iota(jnp.int32, (MERGED, HD), 1)
        == lax.broadcasted_iota(jnp.int32, (MERGED, HD), 0) + MERGED * lax.axis_index(GROUP),
        counts,
        0.0,
    )
    count_rows = jnp.broadcast_to(jnp.sum(spread, axis=0, keepdims=True), (MERGED, HD)).astype(jnp.bfloat16)
    for side in range(2):
        exponents[side].wait()
        scaling = jnp.exp2(exps[side].astype(jnp.float32))
        for head in range(heads):
            if head * chunks % heads == 0:
                sides[side][head * chunks // heads].wait()
            chosen = (onehot * scaling[head : head + 1, :]).astype(jnp.bfloat16)
            start = (side * heads + head) * MERGED
            sums[start : start + MERGED, :] = jnp.dot(
                chosen, held[side, :, head * HD : (head + 1) * HD], preferred_element_type=jnp.float32
            )
    rotated = jnp.dot(
        sums[...], table, precision=lax.Precision.HIGHEST, preferred_element_type=jnp.float32
    ).reshape(2, heads, MERGED, HD)
    merged = (rotated / counts[None, None, :, :] * SCALE).astype(jnp.bfloat16)
    pair = out_ref.shape[1] // (2 * MERGED)
    for head in range(heads):
        target, place = head // pair, head % pair * 2 * MERGED
        out_ref[target, place : place + MERGED, :] = merged[0, head]
        out_ref[target, place + MERGED : place + 2 * MERGED, :] = merged[1, head]
    for target in range(heads // pair):
        out_ref[target, pair * 2 * MERGED :, :] = count_rows


def prepare_merged(key, value, key_exp, value_exp, merge_map, targets, chunks=2):
    heads = key_exp.shape[0]
    rows = heads // targets * 2 * MERGED + MERGED
    merge_map = merge_map.reshape(1, -1)
    return pl.pallas_call(
        lambda *refs: prepare_merged_kernel(chunks, *refs),
        in_specs=[pl.BlockSpec(memory_space=pl.ANY)] * 5,
        out_specs=pl.BlockSpec(memory_space=pltpu.VMEM),
        out_shape=pltpu.VMEM((targets, rows, HD), jnp.bfloat16),
        scratch_shapes=[
            pltpu.VMEM((2 * heads * MERGED, HD), jnp.float32),
            pltpu.VMEM((2, *key.shape), jnp.bfloat16),
            pltpu.VMEM((2, *key_exp.shape), jnp.int32),
            pltpu.VMEM(merge_map.shape, jnp.int32),
            pltpu.SemaphoreType.DMA((2, chunks)),
            pltpu.SemaphoreType.DMA((3,)),
        ],
        compiler_params=pltpu.CompilerParams(vmem_limit_bytes=56 * 2**20),
        cost_estimate=pl.CostEstimate(flops=2**27, bytes_accessed=2**21, transcendentals=0),
        name="prepare_merged",
    )(key, value, key_exp, value_exp, merge_map)


def prepare_queries_kernel(chunks, query_ref, exp_ref, out_ref, held, exps, arrived, small):
    heads = exps.shape[0]
    exponents = pltpu.make_async_copy(exp_ref, exps, small.at[0])
    copies = columns_of(query_ref, held, arrived, chunks)
    exponents.start()
    for copy in copies:
        copy.start()
    table = sylvester().astype(jnp.bfloat16)
    exponents.wait()
    scaling = (jnp.exp2(exps[...].astype(jnp.float32)) * SCALE).T
    for head in range(heads):
        if head * chunks % heads == 0:
            copies[head * chunks // heads].wait()
        rotated = jnp.dot(
            held[:, head * HD : (head + 1) * HD], table, preferred_element_type=jnp.float32
        )
        out_ref[head] = (rotated * scaling[:, head : head + 1]).astype(jnp.bfloat16)


def prepare_queries(query, query_exp, chunks=2):
    tokens = query.shape[0]
    heads = query_exp.shape[0]
    return pl.pallas_call(
        lambda *refs: prepare_queries_kernel(chunks, *refs),
        in_specs=[pl.BlockSpec(memory_space=pl.ANY)] * 2,
        out_specs=pl.BlockSpec(memory_space=pltpu.VMEM),
        out_shape=pltpu.VMEM((heads, tokens, HD), jnp.bfloat16),
        scratch_shapes=[
            pltpu.VMEM(query.shape, jnp.bfloat16),
            pltpu.VMEM(query_exp.shape, jnp.int32),
            pltpu.SemaphoreType.DMA((chunks,)),
            pltpu.SemaphoreType.DMA((1,)),
        ],
        compiler_params=pltpu.CompilerParams(vmem_limit_bytes=56 * 2**20),
        cost_estimate=pl.CostEstimate(flops=2**27, bytes_accessed=2**21, transcendentals=0),
        name="prepare_queries",
    )(query, query_exp)


def repack_kernel(in_ref, out_ref):
    sources, height, _ = in_ref.shape
    rows = sources * MERGED
    for kind in range(height // MERGED - 1):
        out_ref[0, kind * rows : (kind + 1) * rows, :] = in_ref[
            :, kind * MERGED : (kind + 1) * MERGED, :
        ].reshape(rows, HD)
    counts = jnp.sum(in_ref[:, height - MERGED :, :].astype(jnp.float32), axis=0)
    out_ref[0, (height // MERGED - 1) * rows :, :] = jnp.concatenate([counts] * 2, axis=0).astype(jnp.bfloat16)


def repack(received):
    sources, height, _ = received.shape
    rows = sources * MERGED
    return pl.pallas_call(
        repack_kernel,
        out_shape=jax.ShapeDtypeStruct((1, (height // MERGED - 1) * rows + 16, HD), jnp.bfloat16),
        compiler_params=pltpu.CompilerParams(vmem_limit_bytes=4 * 2**20),
        cost_estimate=pl.CostEstimate(flops=2**20, bytes_accessed=2**18, transcendentals=0),
        name="repack",
    )(received)


def attend_kernel(parts, first, last, sub, *refs):
    query_ref = refs[0]
    piece_refs = refs[1 : 1 + parts]
    refs = refs[1 + parts :]
    if not first:
        both_ref, top_ref = refs[:2]
        refs = refs[2:]
    out_refs = refs[: 1 if last else 2]
    keys, values, logs = refs[1 if last else 2 :]
    sources, pair, tokens, _ = query_ref.shape
    step = sub // tokens
    place = 0
    for piece_ref in piece_refs:
        for block in range(piece_ref.shape[0]):
            for head in range(pair):
                base = head * 2 * HD
                keys[head, place : place + HD, :] = piece_ref[block, base : base + HD, :]
                values[head, place : place + HD, 0:HD] = piece_ref[block, base + HD : base + 2 * HD, :]
            counts = piece_ref[block, 2 * pair * HD : 2 * pair * HD + 16, :].astype(jnp.float32)
            logs[:, place : place + HD] = jnp.log(counts[0:8]) * LOG2E
            place += HD
    values[:, :, HD:] = jnp.ones((pair, place, HD), jnp.bfloat16)

    def score(head, index):
        scores = lax.dot_general(
            query_ref[index * step : (index + 1) * step, head].reshape(sub, HD),
            keys[head],
            (((1,), (1,)), ((), ())),
            preferred_element_type=jnp.float32,
        )
        return scores * (SCALE * LOG2E) + logs[0:1, :]

    def mix(head, index, scores):
        rows = slice(index * sub, (index + 1) * sub)
        top = jnp.broadcast_to(jnp.max(scores, axis=1, keepdims=True), (sub, HD))
        if not first:
            before = top_ref[head, rows, :]
            top = jnp.maximum(top, before)
            rescale = jnp.exp2(before - top)
        weights = jnp.exp2(scores - jnp.concatenate([top] * (place // HD), axis=1)).astype(jnp.bfloat16)
        both = jnp.dot(weights, values[head], preferred_element_type=jnp.float32)
        if not first:
            both = both + both_ref[head, rows, :] * jnp.concatenate([rescale] * 2, axis=1)
        if last:
            done = (both[:, 0:HD] / both[:, HD:]).astype(jnp.bfloat16)
            out_refs[0][index * step : (index + 1) * step, head] = done.reshape(step, tokens, HD)
        else:
            out_refs[0][head, rows, :] = both
            out_refs[1][head, rows, :] = top

    tiles = [(head, index) for head in range(pair) for index in range(sources // step)]
    upcoming = score(*tiles[0])
    for number, tile in enumerate(tiles):
        scores = upcoming
        if number + 1 < len(tiles):
            upcoming = score(*tiles[number + 1])
        mix(*tile, scores)


def attend(queries, pieces, state, last, sub=256):
    sources, pair, tokens, _ = queries.shape
    rows = sources * tokens
    parts = len(pieces)
    slots = HD * sum(piece.shape[0] for piece in pieces)
    first = state is None
    if last:
        out_shape = jax.ShapeDtypeStruct(queries.shape, jnp.bfloat16)
    else:
        out_shape = [jax.ShapeDtypeStruct((pair, rows, width), jnp.float32) for width in (2 * HD, HD)]
    return pl.pallas_call(
        lambda *refs: attend_kernel(parts, first, last, sub, *refs),
        out_shape=out_shape,
        scratch_shapes=[
            pltpu.VMEM((pair, slots, HD), jnp.bfloat16),
            pltpu.VMEM((pair, slots, 2 * HD), jnp.bfloat16),
            pltpu.VMEM((8, slots), jnp.float32),
        ],
        compiler_params=pltpu.CompilerParams(vmem_limit_bytes=24 * 2**20),
        cost_estimate=pl.CostEstimate(
            flops=8 * pair * rows * slots * HD,
            bytes_accessed=16 * pair * rows * HD,
            transcendentals=pair * rows * slots,
        ),
        name="attend",
    )(queries, *pieces, *(() if first else state))


def place(zh, ya, yb, core, rep):
    return (((zh % ZH * (Y // 2) + ya % (Y // 2)) * 2 + yb) * CORE + core) * REP + rep


def ring(by, over_y):
    pairs = []
    for zh, ya, yb, core, rep in np.ndindex(ZH, Y // 2, 2, CORE, REP):
        if core == over_y:
            moved = (zh, ya + (by if yb == 0 else -by))
        else:
            moved = (zh + (by if rep == 0 else -by), ya)
        pairs.append((place(zh, ya, yb, core, rep), place(*moved, yb, core, rep)))
    return pairs


def first_ring(by):
    return ring(by, 1)


def second_ring(by):
    return ring(by, 0)


def per_device(
    query_mantissa,
    key_mantissa,
    value_mantissa,
    query_exponent,
    key_exponent,
    value_exponent,
    merge_map,
):
    tokens = query_mantissa.shape[0]
    heads = query_exponent.shape[1]
    targets = lax.axis_size(GROUP)
    merged = prepare_merged(key_mantissa, value_mantissa, key_exponent.T, value_exponent.T, merge_map, targets)
    queries = prepare_queries(query_mantissa, query_exponent.T)
    received = lax.all_to_all(merged, GROUP, split_axis=0, concat_axis=0, tiled=True)
    received, queries = lax.optimization_barrier((received, queries))
    own = repack(received)
    queries, own = lax.optimization_barrier((queries, own))
    head_queries = lax.all_to_all(queries, GROUP, split_axis=0, concat_axis=0, tiled=True)
    head_queries = head_queries.reshape(targets, heads // targets, tokens, HD)
    near = jnp.concatenate([own] + [lax.ppermute(own, RING, first_ring(by)) for by in (1, -1, 2)], axis=0)
    up = lax.ppermute(near, RING, second_ring(1))
    down = lax.ppermute(near, RING, second_ring(-1))
    state = attend(head_queries, (near,), None, False)
    up, state = lax.optimization_barrier((up, state))
    far = lax.ppermute(up, RING, second_ring(1))
    state = attend(head_queries, (up, down), state, False)
    attended = attend(head_queries, (far,), state, True)
    returned = lax.all_to_all(
        attended.reshape(heads, tokens, HD), GROUP, split_axis=0, concat_axis=0, tiled=True
    )
    return jnp.transpose(returned, (1, 0, 2)).reshape(tokens, heads * HD)


def solution(mesh):
    fine = Mesh(mesh.devices.reshape(ZH, Y // 2, 2, X, CORE, 2), ("zh", "yA", "yB", "x", "core", "rep"))
    tokens = P(("rep", "zh", "yA", "yB", "x", "core"), None)
    return jax.shard_map(
        per_device,
        mesh=fine,
        in_specs=(tokens,) * 6 + (P(("rep", "zh", "yA", "yB", "x", "core")),),
        out_specs=tokens,
        check_vma=False,
    )
```

```python
import math

import jax
import jax.numpy as jnp
import numpy as np
from jax import lax
from jax.experimental import pallas as pl
from jax.experimental.pallas import tpu as pltpu
from jax.sharding import Mesh
from jax.sharding import PartitionSpec as P

HD = 128
MERGED = 8
ZH, Y, X, CORE = 4, 8, 4, 2
GROUP = ("yB", "x", "core")
RING = ("zh", "yA", "yB", "core", "rep")
REP = 2
SCALE = 1.0 / math.sqrt(HD)
LOG2E = math.log2(math.e)


def sylvester():
    row = lax.broadcasted_iota(jnp.int32, (HD, HD), 0)
    column = lax.broadcasted_iota(jnp.int32, (HD, HD), 1)
    both = row & column
    odd = both
    for bit in range(1, HD.bit_length() - 1):
        odd = odd ^ (both >> bit)
    return (1 - 2 * (odd & 1)).astype(jnp.float32)


def columns_of(source, held, arrived, chunks):
    piece = held.shape[1] // chunks
    copies = []
    for chunk in range(chunks):
        columns = pl.ds(chunk * piece, piece)
        copies.append(pltpu.make_async_copy(source.at[:, columns], held.at[:, columns], arrived.at[chunk]))
    return copies


def prepare_merged_kernel(
    chunks, key_ref, value_ref, key_exp_ref, value_exp_ref, map_ref, out_ref, sums, held, exps, where, arrived, small
):
    tokens, width = held.shape[1:]
    heads = width // HD
    exponents = [
        pltpu.make_async_copy(key_exp_ref, exps.at[0], small.at[0]),
        pltpu.make_async_copy(value_exp_ref, exps.at[1], small.at[1]),
    ]
    mapped = pltpu.make_async_copy(map_ref, where, small.at[2])
    sides = [
        columns_of(source, held.at[side], arrived.at[side], chunks)
        for side, source in enumerate((key_ref, value_ref))
    ]
    mapped.start()
    exponents[0].start()
    for copy in sides[0]:
        copy.start()
    exponents[1].start()
    for copy in sides[1]:
        copy.start()
    table = sylvester()
    mapped.wait()
    slot = lax.broadcasted_iota(jnp.int32, (MERGED, tokens), 0)
    onehot = (where[...] == slot).astype(jnp.float32)
    counts = jnp.sum(onehot, axis=1, keepdims=True)
    spread = jnp.where(
        lax.broadcasted_iota(jnp.int32, (MERGED, HD), 1)
        == lax.broadcasted_iota(jnp.int32, (MERGED, HD), 0) + MERGED * lax.axis_index(GROUP),
        counts,
        0.0,
    )
    count_rows = jnp.broadcast_to(jnp.sum(spread, axis=0, keepdims=True), (MERGED, HD)).astype(jnp.bfloat16)
    for side in range(2):
        exponents[side].wait()
        scaling = jnp.exp2(exps[side].astype(jnp.float32))
        for head in range(heads):
            if head * chunks % heads == 0:
                sides[side][head * chunks // heads].wait()
            chosen = (onehot * scaling[head : head + 1, :]).astype(jnp.bfloat16)
            start = (side * heads + head) * MERGED
            sums[start : start + MERGED, :] = jnp.dot(
                chosen, held[side, :, head * HD : (head + 1) * HD], preferred_element_type=jnp.float32
            )
    rotated = jnp.dot(
        sums[...], table, precision=lax.Precision.HIGHEST, preferred_element_type=jnp.float32
    ).reshape(2, heads, MERGED, HD)
    merged = (rotated / counts[None, None, :, :] * SCALE).astype(jnp.bfloat16)
    pair = out_ref.shape[1] // (2 * MERGED)
    for head in range(heads):
        target, place = head // pair, head % pair * 2 * MERGED
        out_ref[target, place : place + MERGED, :] = merged[0, head]
        out_ref[target, place + MERGED : place + 2 * MERGED, :] = merged[1, head]
    for target in range(heads // pair):
        out_ref[target, pair * 2 * MERGED :, :] = count_rows


def prepare_merged(key, value, key_exp, value_exp, merge_map, targets, chunks=2):
    heads = key_exp.shape[0]
    rows = heads // targets * 2 * MERGED + MERGED
    merge_map = merge_map.reshape(1, -1)
    return pl.pallas_call(
        lambda *refs: prepare_merged_kernel(chunks, *refs),
        in_specs=[pl.BlockSpec(memory_space=pl.ANY)] * 5,
        out_specs=pl.BlockSpec(memory_space=pltpu.VMEM),
        out_shape=pltpu.VMEM((targets, rows, HD), jnp.bfloat16),
        scratch_shapes=[
            pltpu.VMEM((2 * heads * MERGED, HD), jnp.float32),
            pltpu.VMEM((2, *key.shape), jnp.bfloat16),
            pltpu.VMEM((2, *key_exp.shape), jnp.int32),
            pltpu.VMEM(merge_map.shape, jnp.int32),
            pltpu.SemaphoreType.DMA((2, chunks)),
            pltpu.SemaphoreType.DMA((3,)),
        ],
        compiler_params=pltpu.CompilerParams(vmem_limit_bytes=56 * 2**20),
        cost_estimate=pl.CostEstimate(flops=2**27, bytes_accessed=2**21, transcendentals=0),
        name="prepare_merged",
    )(key, value, key_exp, value_exp, merge_map)


def prepare_queries_kernel(chunks, query_ref, exp_ref, out_ref, held, exps, arrived, small):
    heads = exps.shape[0]
    exponents = pltpu.make_async_copy(exp_ref, exps, small.at[0])
    copies = columns_of(query_ref, held, arrived, chunks)
    exponents.start()
    for copy in copies:
        copy.start()
    table = sylvester().astype(jnp.bfloat16)
    exponents.wait()
    scaling = (jnp.exp2(exps[...].astype(jnp.float32)) * SCALE).T
    for head in range(heads):
        if head * chunks % heads == 0:
            copies[head * chunks // heads].wait()
        rotated = jnp.dot(
            held[:, head * HD : (head + 1) * HD], table, preferred_element_type=jnp.float32
        )
        out_ref[head] = (rotated * scaling[:, head : head + 1]).astype(jnp.bfloat16)


def prepare_queries(query, query_exp, chunks=2):
    tokens = query.shape[0]
    heads = query_exp.shape[0]
    return pl.pallas_call(
        lambda *refs: prepare_queries_kernel(chunks, *refs),
        in_specs=[pl.BlockSpec(memory_space=pl.ANY)] * 2,
        out_specs=pl.BlockSpec(memory_space=pltpu.VMEM),
        out_shape=pltpu.VMEM((heads, tokens, HD), jnp.bfloat16),
        scratch_shapes=[
            pltpu.VMEM(query.shape, jnp.bfloat16),
            pltpu.VMEM(query_exp.shape, jnp.int32),
            pltpu.SemaphoreType.DMA((chunks,)),
            pltpu.SemaphoreType.DMA((1,)),
        ],
        compiler_params=pltpu.CompilerParams(vmem_limit_bytes=56 * 2**20),
        cost_estimate=pl.CostEstimate(flops=2**27, bytes_accessed=2**21, transcendentals=0),
        name="prepare_queries",
    )(query, query_exp)


def repack_kernel(in_ref, out_ref):
    sources, height, _ = in_ref.shape
    rows = sources * MERGED
    for kind in range(height // MERGED - 1):
        out_ref[0, kind * rows : (kind + 1) * rows, :] = in_ref[
            :, kind * MERGED : (kind + 1) * MERGED, :
        ].reshape(rows, HD)
    counts = jnp.sum(in_ref[:, height - MERGED :, :].astype(jnp.float32), axis=0)
    out_ref[0, (height // MERGED - 1) * rows :, :] = jnp.concatenate([counts] * 2, axis=0).astype(jnp.bfloat16)


def repack(received):
    sources, height, _ = received.shape
    rows = sources * MERGED
    return pl.pallas_call(
        repack_kernel,
        out_shape=jax.ShapeDtypeStruct((1, (height // MERGED - 1) * rows + 16, HD), jnp.bfloat16),
        compiler_params=pltpu.CompilerParams(vmem_limit_bytes=4 * 2**20),
        cost_estimate=pl.CostEstimate(flops=2**20, bytes_accessed=2**18, transcendentals=0),
        name="repack",
    )(received)


def attend_kernel(parts, first, last, sub, *refs):
    query_ref = refs[0]
    piece_refs = refs[1 : 1 + parts]
    refs = refs[1 + parts :]
    if not first:
        both_ref, top_ref = refs[:2]
        refs = refs[2:]
    out_refs = refs[: 1 if last else 2]
    keys, values, logs = refs[1 if last else 2 :]
    sources, pair, tokens, _ = query_ref.shape
    step = sub // tokens
    place = 0
    for piece_ref in piece_refs:
        for block in range(piece_ref.shape[0]):
            for head in range(pair):
                base = head * 2 * HD
                keys[head, place : place + HD, :] = piece_ref[block, base : base + HD, :]
                values[head, place : place + HD, 0:HD] = piece_ref[block, base + HD : base + 2 * HD, :]
            counts = piece_ref[block, 2 * pair * HD : 2 * pair * HD + 16, :].astype(jnp.float32)
            logs[:, place : place + HD] = jnp.log(counts[0:8]) * LOG2E
            place += HD
    values[:, :, HD:] = jnp.ones((pair, place, HD), jnp.bfloat16)

    def score(head, index):
        scores = lax.dot_general(
            query_ref[index * step : (index + 1) * step, head].reshape(sub, HD),
            keys[head],
            (((1,), (1,)), ((), ())),
            preferred_element_type=jnp.float32,
        )
        return scores * (SCALE * LOG2E) + logs[0:1, :]

    def mix(head, index, scores):
        rows = slice(index * sub, (index + 1) * sub)
        top = jnp.broadcast_to(jnp.max(scores, axis=1, keepdims=True), (sub, HD))
        if not first:
            before = top_ref[head, rows, :]
            top = jnp.maximum(top, before)
            rescale = jnp.exp2(before - top)
        weights = jnp.exp2(scores - jnp.concatenate([top] * (place // HD), axis=1)).astype(jnp.bfloat16)
        both = jnp.dot(weights, values[head], preferred_element_type=jnp.float32)
        if not first:
            both = both + both_ref[head, rows, :] * jnp.concatenate([rescale] * 2, axis=1)
        if last:
            done = (both[:, 0:HD] / both[:, HD:]).astype(jnp.bfloat16)
            out_refs[0][index * step : (index + 1) * step, head] = done.reshape(step, tokens, HD)
        else:
            out_refs[0][head, rows, :] = both
            out_refs[1][head, rows, :] = top

    tiles = [(head, index) for head in range(pair) for index in range(sources // step)]
    upcoming = score(*tiles[0])
    for number, tile in enumerate(tiles):
        scores = upcoming
        if number + 1 < len(tiles):
            upcoming = score(*tiles[number + 1])
        mix(*tile, scores)


def attend(queries, pieces, state, last, sub=256):
    sources, pair, tokens, _ = queries.shape
    rows = sources * tokens
    parts = len(pieces)
    slots = HD * sum(piece.shape[0] for piece in pieces)
    first = state is None
    if last:
        out_shape = jax.ShapeDtypeStruct(queries.shape, jnp.bfloat16)
    else:
        out_shape = [jax.ShapeDtypeStruct((pair, rows, width), jnp.float32) for width in (2 * HD, HD)]
    return pl.pallas_call(
        lambda *refs: attend_kernel(parts, first, last, sub, *refs),
        out_shape=out_shape,
        scratch_shapes=[
            pltpu.VMEM((pair, slots, HD), jnp.bfloat16),
            pltpu.VMEM((pair, slots, 2 * HD), jnp.bfloat16),
            pltpu.VMEM((8, slots), jnp.float32),
        ],
        compiler_params=pltpu.CompilerParams(vmem_limit_bytes=24 * 2**20),
        cost_estimate=pl.CostEstimate(
            flops=8 * pair * rows * slots * HD,
            bytes_accessed=16 * pair * rows * HD,
            transcendentals=pair * rows * slots,
        ),
        name="attend",
    )(queries, *pieces, *(() if first else state))


def place(zh, ya, yb, core, rep):
    return (((zh % ZH * (Y // 2) + ya % (Y // 2)) * 2 + yb) * CORE + core) * REP + rep


def ring(by, over_y):
    pairs = []
    for zh, ya, yb, core, rep in np.ndindex(ZH, Y // 2, 2, CORE, REP):
        if core == over_y:
            moved = (zh, ya + (by if yb == 0 else -by))
        else:
            moved = (zh + (by if rep == 0 else -by), ya)
        pairs.append((place(zh, ya, yb, core, rep), place(*moved, yb, core, rep)))
    return pairs


def first_ring(by):
    return ring(by, 1)


def second_ring(by):
    return ring(by, 0)


def per_device(
    query_mantissa,
    key_mantissa,
    value_mantissa,
    query_exponent,
    key_exponent,
    value_exponent,
    merge_map,
):
    tokens = query_mantissa.shape[0]
    heads = query_exponent.shape[1]
    targets = lax.axis_size(GROUP)
    merged = prepare_merged(key_mantissa, value_mantissa, key_exponent.T, value_exponent.T, merge_map, targets)
    queries = prepare_queries(query_mantissa, query_exponent.T)
    received = lax.all_to_all(merged, GROUP, split_axis=0, concat_axis=0, tiled=True)
    received, queries = lax.optimization_barrier((received, queries))
    own = repack(received)
    queries, own = lax.optimization_barrier((queries, own))
    head_queries = lax.all_to_all(queries, GROUP, split_axis=0, concat_axis=0, tiled=True)
    head_queries = head_queries.reshape(targets, heads // targets, tokens, HD)
    near = jnp.concatenate([own] + [lax.ppermute(own, RING, first_ring(by)) for by in (2, -1, 1)], axis=0)
    up = lax.ppermute(near, RING, second_ring(1))
    down = lax.ppermute(near, RING, second_ring(-1))
    state = attend(head_queries, (near,), None, False)
    up, state = lax.optimization_barrier((up, state))
    far = lax.ppermute(up, RING, second_ring(1))
    state = attend(head_queries, (up, down), state, False)
    attended = attend(head_queries, (far,), state, True)
    returned = lax.all_to_all(
        attended.reshape(heads, tokens, HD), GROUP, split_axis=0, concat_axis=0, tiled=True
    )
    return jnp.transpose(returned, (1, 0, 2)).reshape(tokens, heads * HD)


def solution(mesh):
    fine = Mesh(mesh.devices.reshape(ZH, Y // 2, 2, X, CORE, 2), ("zh", "yA", "yB", "x", "core", "rep"))
    tokens = P(("rep", "zh", "yA", "yB", "x", "core"), None)
    return jax.shard_map(
        per_device,
        mesh=fine,
        in_specs=(tokens,) * 6 + (P(("rep", "zh", "yA", "yB", "x", "core")),),
        out_specs=tokens,
        check_vma=False,
    )
```

```python
import math

import jax
import jax.numpy as jnp
import numpy as np
from jax import lax
from jax.experimental import pallas as pl
from jax.experimental.pallas import tpu as pltpu
from jax.sharding import Mesh
from jax.sharding import PartitionSpec as P

HD = 128
MERGED = 8
ZH, Y, X, CORE = 4, 8, 4, 2
GROUP = ("core", "x", "yB")
RING = ("zh", "yA", "yB", "core", "rep")
REP = 2
SCALE = 1.0 / math.sqrt(HD)
LOG2E = math.log2(math.e)


def sylvester():
    row = lax.broadcasted_iota(jnp.int32, (HD, HD), 0)
    column = lax.broadcasted_iota(jnp.int32, (HD, HD), 1)
    both = row & column
    odd = both
    for bit in range(1, HD.bit_length() - 1):
        odd = odd ^ (both >> bit)
    return (1 - 2 * (odd & 1)).astype(jnp.float32)


def columns_of(source, held, arrived, chunks):
    piece = held.shape[1] // chunks
    copies = []
    for chunk in range(chunks):
        columns = pl.ds(chunk * piece, piece)
        copies.append(pltpu.make_async_copy(source.at[:, columns], held.at[:, columns], arrived.at[chunk]))
    return copies


def prepare_merged_kernel(
    chunks, key_ref, value_ref, key_exp_ref, value_exp_ref, map_ref, out_ref, sums, held, exps, where, arrived, small
):
    tokens, width = held.shape[1:]
    heads = width // HD
    exponents = [
        pltpu.make_async_copy(key_exp_ref, exps.at[0], small.at[0]),
        pltpu.make_async_copy(value_exp_ref, exps.at[1], small.at[1]),
    ]
    mapped = pltpu.make_async_copy(map_ref, where, small.at[2])
    sides = [
        columns_of(source, held.at[side], arrived.at[side], chunks)
        for side, source in enumerate((key_ref, value_ref))
    ]
    mapped.start()
    exponents[0].start()
    for copy in sides[0]:
        copy.start()
    exponents[1].start()
    for copy in sides[1]:
        copy.start()
    table = sylvester()
    mapped.wait()
    slot = lax.broadcasted_iota(jnp.int32, (MERGED, tokens), 0)
    onehot = (where[...] == slot).astype(jnp.float32)
    counts = jnp.sum(onehot, axis=1, keepdims=True)
    spread = jnp.where(
        lax.broadcasted_iota(jnp.int32, (MERGED, HD), 1)
        == lax.broadcasted_iota(jnp.int32, (MERGED, HD), 0) + MERGED * lax.axis_index(GROUP),
        counts,
        0.0,
    )
    count_rows = jnp.broadcast_to(jnp.sum(spread, axis=0, keepdims=True), (MERGED, HD)).astype(jnp.bfloat16)
    for side in range(2):
        exponents[side].wait()
        scaling = jnp.exp2(exps[side].astype(jnp.float32))
        for head in range(heads):
            if head * chunks % heads == 0:
                sides[side][head * chunks // heads].wait()
            chosen = (onehot * scaling[head : head + 1, :]).astype(jnp.bfloat16)
            start = (side * heads + head) * MERGED
            sums[start : start + MERGED, :] = jnp.dot(
                chosen, held[side, :, head * HD : (head + 1) * HD], preferred_element_type=jnp.float32
            )
    rotated = jnp.dot(
        sums[...], table, precision=lax.Precision.HIGHEST, preferred_element_type=jnp.float32
    ).reshape(2, heads, MERGED, HD)
    merged = (rotated / counts[None, None, :, :] * SCALE).astype(jnp.bfloat16)
    pair = out_ref.shape[1] // (2 * MERGED)
    for head in range(heads):
        target, place = head // pair, head % pair * 2 * MERGED
        out_ref[target, place : place + MERGED, :] = merged[0, head]
        out_ref[target, place + MERGED : place + 2 * MERGED, :] = merged[1, head]
    for target in range(heads // pair):
        out_ref[target, pair * 2 * MERGED :, :] = count_rows


def prepare_merged(key, value, key_exp, value_exp, merge_map, targets, chunks=2):
    heads = key_exp.shape[0]
    rows = heads // targets * 2 * MERGED + MERGED
    merge_map = merge_map.reshape(1, -1)
    return pl.pallas_call(
        lambda *refs: prepare_merged_kernel(chunks, *refs),
        in_specs=[pl.BlockSpec(memory_space=pl.ANY)] * 5,
        out_specs=pl.BlockSpec(memory_space=pltpu.VMEM),
        out_shape=pltpu.VMEM((targets, rows, HD), jnp.bfloat16),
        scratch_shapes=[
            pltpu.VMEM((2 * heads * MERGED, HD), jnp.float32),
            pltpu.VMEM((2, *key.shape), jnp.bfloat16),
            pltpu.VMEM((2, *key_exp.shape), jnp.int32),
            pltpu.VMEM(merge_map.shape, jnp.int32),
            pltpu.SemaphoreType.DMA((2, chunks)),
            pltpu.SemaphoreType.DMA((3,)),
        ],
        compiler_params=pltpu.CompilerParams(vmem_limit_bytes=56 * 2**20),
        cost_estimate=pl.CostEstimate(flops=2**27, bytes_accessed=2**21, transcendentals=0),
        name="prepare_merged",
    )(key, value, key_exp, value_exp, merge_map)


def prepare_queries_kernel(chunks, query_ref, exp_ref, out_ref, held, exps, arrived, small):
    heads = exps.shape[0]
    exponents = pltpu.make_async_copy(exp_ref, exps, small.at[0])
    copies = columns_of(query_ref, held, arrived, chunks)
    exponents.start()
    for copy in copies:
        copy.start()
    table = sylvester().astype(jnp.bfloat16)
    exponents.wait()
    scaling = (jnp.exp2(exps[...].astype(jnp.float32)) * SCALE).T
    for head in range(heads):
        if head * chunks % heads == 0:
            copies[head * chunks // heads].wait()
        rotated = jnp.dot(
            held[:, head * HD : (head + 1) * HD], table, preferred_element_type=jnp.float32
        )
        out_ref[head] = (rotated * scaling[:, head : head + 1]).astype(jnp.bfloat16)


def prepare_queries(query, query_exp, chunks=2):
    tokens = query.shape[0]
    heads = query_exp.shape[0]
    return pl.pallas_call(
        lambda *refs: prepare_queries_kernel(chunks, *refs),
        in_specs=[pl.BlockSpec(memory_space=pl.ANY)] * 2,
        out_specs=pl.BlockSpec(memory_space=pltpu.VMEM),
        out_shape=pltpu.VMEM((heads, tokens, HD), jnp.bfloat16),
        scratch_shapes=[
            pltpu.VMEM(query.shape, jnp.bfloat16),
            pltpu.VMEM(query_exp.shape, jnp.int32),
            pltpu.SemaphoreType.DMA((chunks,)),
            pltpu.SemaphoreType.DMA((1,)),
        ],
        compiler_params=pltpu.CompilerParams(vmem_limit_bytes=56 * 2**20),
        cost_estimate=pl.CostEstimate(flops=2**27, bytes_accessed=2**21, transcendentals=0),
        name="prepare_queries",
    )(query, query_exp)


def repack_kernel(in_ref, out_ref):
    sources, height, _ = in_ref.shape
    rows = sources * MERGED
    for kind in range(height // MERGED - 1):
        out_ref[0, kind * rows : (kind + 1) * rows, :] = in_ref[
            :, kind * MERGED : (kind + 1) * MERGED, :
        ].reshape(rows, HD)
    counts = jnp.sum(in_ref[:, height - MERGED :, :].astype(jnp.float32), axis=0)
    out_ref[0, (height // MERGED - 1) * rows :, :] = jnp.concatenate([counts] * 2, axis=0).astype(jnp.bfloat16)


def repack(received):
    sources, height, _ = received.shape
    rows = sources * MERGED
    return pl.pallas_call(
        repack_kernel,
        out_shape=jax.ShapeDtypeStruct((1, (height // MERGED - 1) * rows + 16, HD), jnp.bfloat16),
        compiler_params=pltpu.CompilerParams(vmem_limit_bytes=4 * 2**20),
        cost_estimate=pl.CostEstimate(flops=2**20, bytes_accessed=2**18, transcendentals=0),
        name="repack",
    )(received)


def attend_kernel(parts, first, last, sub, *refs):
    query_ref = refs[0]
    piece_refs = refs[1 : 1 + parts]
    refs = refs[1 + parts :]
    if not first:
        both_ref, top_ref = refs[:2]
        refs = refs[2:]
    out_refs = refs[: 1 if last else 2]
    keys, values, logs = refs[1 if last else 2 :]
    sources, pair, tokens, _ = query_ref.shape
    step = sub // tokens
    place = 0
    for piece_ref in piece_refs:
        for block in range(piece_ref.shape[0]):
            for head in range(pair):
                base = head * 2 * HD
                keys[head, place : place + HD, :] = piece_ref[block, base : base + HD, :]
                values[head, place : place + HD, 0:HD] = piece_ref[block, base + HD : base + 2 * HD, :]
            counts = piece_ref[block, 2 * pair * HD : 2 * pair * HD + 16, :].astype(jnp.float32)
            logs[:, place : place + HD] = jnp.log(counts[0:8]) * LOG2E
            place += HD
    values[:, :, HD:] = jnp.ones((pair, place, HD), jnp.bfloat16)

    def score(head, index):
        scores = lax.dot_general(
            query_ref[index * step : (index + 1) * step, head].reshape(sub, HD),
            keys[head],
            (((1,), (1,)), ((), ())),
            preferred_element_type=jnp.float32,
        )
        return scores * (SCALE * LOG2E) + logs[0:1, :]

    def mix(head, index, scores):
        rows = slice(index * sub, (index + 1) * sub)
        top = jnp.broadcast_to(jnp.max(scores, axis=1, keepdims=True), (sub, HD))
        if not first:
            before = top_ref[head, rows, :]
            top = jnp.maximum(top, before)
            rescale = jnp.exp2(before - top)
        weights = jnp.exp2(scores - jnp.concatenate([top] * (place // HD), axis=1)).astype(jnp.bfloat16)
        both = jnp.dot(weights, values[head], preferred_element_type=jnp.float32)
        if not first:
            both = both + both_ref[head, rows, :] * jnp.concatenate([rescale] * 2, axis=1)
        if last:
            done = (both[:, 0:HD] / both[:, HD:]).astype(jnp.bfloat16)
            out_refs[0][index * step : (index + 1) * step, head] = done.reshape(step, tokens, HD)
        else:
            out_refs[0][head, rows, :] = both
            out_refs[1][head, rows, :] = top

    tiles = [(head, index) for head in range(pair) for index in range(sources // step)]
    upcoming = score(*tiles[0])
    for number, tile in enumerate(tiles):
        scores = upcoming
        if number + 1 < len(tiles):
            upcoming = score(*tiles[number + 1])
        mix(*tile, scores)


def attend(queries, pieces, state, last, sub=256):
    sources, pair, tokens, _ = queries.shape
    rows = sources * tokens
    parts = len(pieces)
    slots = HD * sum(piece.shape[0] for piece in pieces)
    first = state is None
    if last:
        out_shape = jax.ShapeDtypeStruct(queries.shape, jnp.bfloat16)
    else:
        out_shape = [jax.ShapeDtypeStruct((pair, rows, width), jnp.float32) for width in (2 * HD, HD)]
    return pl.pallas_call(
        lambda *refs: attend_kernel(parts, first, last, sub, *refs),
        out_shape=out_shape,
        scratch_shapes=[
            pltpu.VMEM((pair, slots, HD), jnp.bfloat16),
            pltpu.VMEM((pair, slots, 2 * HD), jnp.bfloat16),
            pltpu.VMEM((8, slots), jnp.float32),
        ],
        compiler_params=pltpu.CompilerParams(vmem_limit_bytes=24 * 2**20),
        cost_estimate=pl.CostEstimate(
            flops=8 * pair * rows * slots * HD,
            bytes_accessed=16 * pair * rows * HD,
            transcendentals=pair * rows * slots,
        ),
        name="attend",
    )(queries, *pieces, *(() if first else state))


def place(zh, ya, yb, core, rep):
    return (((zh % ZH * (Y // 2) + ya % (Y // 2)) * 2 + yb) * CORE + core) * REP + rep


def ring(by, over_y):
    pairs = []
    for zh, ya, yb, core, rep in np.ndindex(ZH, Y // 2, 2, CORE, REP):
        if core == over_y:
            moved = (zh, ya + (by if yb == 0 else -by))
        else:
            moved = (zh + (by if rep == 0 else -by), ya)
        pairs.append((place(zh, ya, yb, core, rep), place(*moved, yb, core, rep)))
    return pairs


def first_ring(by):
    return ring(by, 1)


def second_ring(by):
    return ring(by, 0)


def per_device(
    query_mantissa,
    key_mantissa,
    value_mantissa,
    query_exponent,
    key_exponent,
    value_exponent,
    merge_map,
):
    tokens = query_mantissa.shape[0]
    heads = query_exponent.shape[1]
    targets = lax.axis_size(GROUP)
    merged = prepare_merged(key_mantissa, value_mantissa, key_exponent.T, value_exponent.T, merge_map, targets)
    queries = prepare_queries(query_mantissa, query_exponent.T)
    received = lax.all_to_all(merged, GROUP, split_axis=0, concat_axis=0, tiled=True)
    received, queries = lax.optimization_barrier((received, queries))
    own = repack(received)
    queries, own = lax.optimization_barrier((queries, own))
    head_queries = lax.all_to_all(queries, GROUP, split_axis=0, concat_axis=0, tiled=True)
    head_queries = head_queries.reshape(targets, heads // targets, tokens, HD)
    near = jnp.concatenate([own] + [lax.ppermute(own, RING, first_ring(by)) for by in (2, 1, -1)], axis=0)
    up = lax.ppermute(near, RING, second_ring(1))
    down = lax.ppermute(near, RING, second_ring(-1))
    state = attend(head_queries, (near,), None, False)
    up, state = lax.optimization_barrier((up, state))
    far = lax.ppermute(up, RING, second_ring(1))
    state = attend(head_queries, (up, down), state, False)
    attended = attend(head_queries, (far,), state, True)
    returned = lax.all_to_all(
        attended.reshape(heads, tokens, HD), GROUP, split_axis=0, concat_axis=0, tiled=True
    )
    return jnp.transpose(returned, (1, 0, 2)).reshape(tokens, heads * HD)


def solution(mesh):
    fine = Mesh(mesh.devices.reshape(ZH, Y // 2, 2, X, CORE, 2), ("zh", "yA", "yB", "x", "core", "rep"))
    tokens = P(("rep", "zh", "yA", "yB", "x", "core"), None)
    return jax.shard_map(
        per_device,
        mesh=fine,
        in_specs=(tokens,) * 6 + (P(("rep", "zh", "yA", "yB", "x", "core")),),
        out_specs=tokens,
        check_vma=False,
    )
```
